32 devices in a mesh: parts: 2 (over y), shard: 4 (over z), group: 4 (over x, core).
Axes of the slice: x: 2, y: 2, z: 4, core: 2. Of those that a mesh axis runs over, the one named last changes fastest.
Arguments:
- base: bfloat16 [4, 3, 4096, 1536], P('parts', None, 'shard'), parts along dimension 0, may hold values from -6 to 6
- narrow: bfloat16 [64, 3, 4096, 64], P('parts', None, ('shard', 'group')), parts along dimension 0, may hold values from -6 to 6
- wide: bfloat16 [64, 3, 64, 1536], P('parts', None, None, ('shard', 'group')), parts along dimension 0, may hold values from -0.75 to 0.75
- adapted_expert_index: int32 [4], P('parts'), parts along dimension 0, may hold values from 0 to 31, as said below
Outputs:
- merged: bfloat16 [4, 3, 4096, 1536], P('parts', None, 'shard'), parts along dimension 0
The draws below stay inside these ranges and needn't reach their ends.
There are 2 independent parts, one for each index of `parts`. The reference program is written for one: setup_inputs(seed, part) draws one part's arguments, and reference() takes and returns one part's arrays. A program takes and returns all parts, laid end to end along the dimension named above; each array names one. Nothing has to cross between parts.
Inputs may be any that keep to these rules, and one draw needn't show every extreme that they name: `adapted_expert_index`: 2 distinct expert numbers of 0 to 31.
All inputs are finite; a program needn't handle non-finite values.
Results may differ from the reference program's by a relative error of at most 0.001.
Values may be sent and summed in bfloat16 or wider, within the bound.
No kernel may reach another device: no remote copies, remote signals or barrier semaphores. Data moves between devices by JAX's collectives and lax.ppermute only.
A program may use at most 128 MiB of HBM per device.

```python
import jax
import jax.numpy as jnp

D = 4096
F = 1536
R = 64
ADAPTED_EXPERTS = 32
EXPERTS = 2


def draw_adapted_expert_index(key, part):
    key = jax.random.fold_in(key, 7)
    return jax.random.permutation(key, ADAPTED_EXPERTS)[:EXPERTS].astype(jnp.int32)


def steps_of(stream_key, extent, pieces, smallest, largest):
    def one(position, shards_of):
        draws = jax.random.uniform(jax.random.fold_in(jax.random.fold_in(stream_key, 6), position), (shards_of,), jnp.float32, smallest / len(pieces), largest / len(pieces))
        return jnp.repeat(jnp.exp(draws), extent[position] // shards_of).reshape((-1,) + (1,) * (len(extent) - position - 1))

    loudness = one(*pieces[0])
    for cut in pieces[1:]:
        loudness = loudness * one(*cut)
    return loudness


def scatter_about(key, dims, spread, reach, pieces=(), kind=jnp.bfloat16):
    drawn = jax.random.normal(key, dims, jnp.float32) * spread
    if len(pieces) > 0:
        drawn = steps_of(key, dims, pieces, -0.22, 0.18) * drawn
    return jnp.clip(drawn, min=-reach, max=reach).astype(kind)


def setup_inputs(seed: int = 0, part: int = 0) -> dict:
    key_list = jax.random.split(jax.random.key(seed), 5)
    part_keys = jax.random.split(jax.random.fold_in(key_list[4], part), 5)
    base = scatter_about(part_keys[0], (EXPERTS, 3, D, F), 1.0, 6.0, ((2, 4),))
    narrow = scatter_about(part_keys[1], (ADAPTED_EXPERTS, 3, D, R), 1.0, 6.0, ((2, 16),))
    wide = scatter_about(part_keys[2], (ADAPTED_EXPERTS, 3, R, F), R ** -0.5, 0.75, ((3, 16),))
    adapted_expert_index = draw_adapted_expert_index(jax.random.fold_in(jax.random.fold_in(key_list[4], part), 71), part)
    return dict(base=base, narrow=narrow, wide=wide, adapted_expert_index=adapted_expert_index)


adapter_scale = 0.5


def reference(base, narrow, wide, adapted_expert_index):
    chosen_narrow = jnp.take(narrow, adapted_expert_index.astype(jnp.int32), axis=0).astype(jnp.float32)
    chosen_wide = jnp.take(wide, adapted_expert_index.astype(jnp.int32), axis=0).astype(jnp.float32)
    adapter_update = jnp.einsum("epdr,eprf->epdf", chosen_narrow, chosen_wide)
    return (base.astype(jnp.float32) + adapter_scale * adapter_update).astype(jnp.bfloat16)
```

```python
import functools

import jax
import jax.numpy as jnp
from jax import lax
from jax.experimental import pallas as pl
from jax.experimental.pallas import tpu as pltpu
from jax.sharding import PartitionSpec as P

adapter_scale = 0.5
out_slots = 4


def select_kernel(index_ref, narrow_ref, wide_ref, n_out, w_out, n_buf, w_buf, sems):
    experts = index_ref.shape[0]
    rank = narrow_ref.shape[2]
    copies = []
    for e in range(experts):
        i = index_ref[e]
        rows = pl.ds(e * rank, rank)
        copies.append(pltpu.make_async_copy(narrow_ref.at[i], n_buf.at[:, rows], sems.at[e, 0]))
        copies.append(pltpu.make_async_copy(wide_ref.at[i], w_buf.at[:, rows], sems.at[e, 1]))
    for copy in copies:
        copy.start()
    for copy in copies:
        copy.wait()
    for p in range(n_buf.shape[0]):
        n = n_buf[p].astype(jnp.float32) * adapter_scale
        n_out[p] = n.T.astype(n_out.dtype)
        w_out[p] = w_buf[p].astype(jnp.float32).T.astype(w_out.dtype)


def select(narrow, wide, index):
    experts = index.shape[0]
    _, projections, rank, rows = narrow.shape
    columns = wide.shape[3]
    deep = experts * rank
    return pl.pallas_call(
        select_kernel,
        out_shape=(
            jax.ShapeDtypeStruct((projections, rows, deep), narrow.dtype),
            jax.ShapeDtypeStruct((projections, columns, deep), wide.dtype),
        ),
        in_specs=[
            pl.BlockSpec(memory_space=pltpu.SMEM),
            pl.BlockSpec(memory_space=pl.ANY),
            pl.BlockSpec(memory_space=pl.ANY),
        ],
        out_specs=[pl.BlockSpec(memory_space=pltpu.VMEM)] * 2,
        scratch_shapes=[
            pltpu.VMEM((projections, deep, rows), narrow.dtype),
            pltpu.VMEM((projections, deep, columns), wide.dtype),
            pltpu.SemaphoreType.DMA((experts, 2)),
        ],
        compiler_params=pltpu.CompilerParams(vmem_limit_bytes=4 * 2**20),
        name="select",
    )(index, narrow, wide)


def merge_kernel(n_order, w_order, rank, *refs):
    base_ref = refs[0]
    n_refs = refs[1 : 1 + len(n_order)]
    w_refs = refs[1 + len(n_order) : 1 + len(n_order) + len(w_order)]
    out_ref, w_all, out_buf, sems = refs[1 + len(n_order) + len(w_order) :]
    experts, projections = base_ref.shape[:2]
    rows = n_refs[0].shape[1]
    columns = w_refs[0].shape[1]
    wide_columns = base_ref.shape[3]
    step_columns = 256 if wide_columns % 256 == 0 else wide_columns
    s, g = lax.axis_index("shard"), lax.axis_index("group")

    for w_ref, place in zip(w_refs, w_order):
        at = pl.multiple_of(place(s, g) * columns, columns)
        for p in range(projections):
            w_all[p, pl.ds(at, columns), :] = w_ref[p]

    lane_expert = lax.broadcasted_iota(jnp.int32, (rows, n_refs[0].shape[2]), 1) // rank
    step = 0
    copies = []
    for p in range(projections):
        for n_ref, place in zip(n_refs, n_order):
            at = pl.multiple_of(place(s, g) * rows, rows)
            for e in range(experts):
                slot = step % out_slots
                if step >= out_slots:
                    copies[step - out_slots].wait()
                n = n_ref[p]
                n = jnp.where(lane_expert == e, n, jnp.zeros_like(n))
                for f in range(0, wide_columns, step_columns):
                    delta = lax.dot_general(
                        n,
                        w_all[p, f : f + step_columns],
                        (((1,), (1,)), ((), ())),
                        preferred_element_type=jnp.float32,
                    )
                    b = base_ref[e, p, pl.ds(at, rows), f : f + step_columns]
                    out_buf[slot, :, f : f + step_columns] = (b.astype(jnp.float32) + delta).astype(out_buf.dtype)
                copy = pltpu.make_async_copy(out_buf.at[slot], out_ref.at[e, p, pl.ds(at, rows)], sems.at[slot])
                copy.start()
                copies.append(copy)
                step += 1
    for copy in copies[max(0, step - out_slots) :]:
        copy.wait()


def merge(base, n_parts, w_parts, n_order, w_order, rank):
    experts, projections, width, wide_columns = base.shape
    _, rows, deep = n_parts[0].shape
    in_vmem = pl.BlockSpec(memory_space=pltpu.VMEM)
    return pl.pallas_call(
        functools.partial(merge_kernel, n_order, w_order, rank),
        out_shape=jax.ShapeDtypeStruct(base.shape, base.dtype),
        in_specs=[in_vmem] * (1 + len(n_parts) + len(w_parts)),
        out_specs=pl.BlockSpec(memory_space=pl.ANY),
        scratch_shapes=[
            pltpu.VMEM((projections, wide_columns, deep), base.dtype),
            pltpu.VMEM((out_slots, rows, wide_columns), base.dtype),
            pltpu.SemaphoreType.DMA((out_slots,)),
        ],
        compiler_params=pltpu.CompilerParams(vmem_limit_bytes=30 * 2**20),
        cost_estimate=pl.CostEstimate(
            flops=2 * base.size * rank, bytes_accessed=4 * base.size, transcendentals=0
        ),
        name="merge",
    )(base, *n_parts, *w_parts)


def on_device(shards, groups, base, narrow, wide, adapted_expert_index):
    rank = narrow.shape[3]
    n, w = select(jnp.swapaxes(narrow, 2, 3), wide, adapted_expert_index)
    axes = ("shard", "group")

    def send(x, shift, flip):
        pairs = []
        for s in range(shards):
            for g in range(groups):
                pairs.append((s * groups + g, (s + shift) % shards * groups + (g ^ flip)))
        return lax.ppermute(x, axes, pairs)

    if groups == 4:
        w_line = [w] + [send(w, shift, 0) for shift in range(1, shards)]
        n_pair = [n, send(n, 0, 2)]
        w_two = w_line + [send(x, 0, 2) for x in w_line]
        n_parts = n_pair + [send(x, 0, 1) for x in n_pair]
        w_parts = w_two + [send(x, 0, 1) for x in w_two]
        n_order = [lambda s, g, m=m: g ^ m for m in (0, 2, 1, 3)]
        w_order = [
            lambda s, g, m=m, k=k: lax.rem(s + (shards - k), shards) * groups + (g ^ m)
            for m in (0, 2, 1, 3)
            for k in range(shards)
        ]
    else:
        n_parts = [lax.all_gather(n, "group", axis=1, tiled=True)]
        w_parts = [lax.all_gather(w, axes, axis=1, tiled=True)]
        n_order = w_order = [lambda s, g: 0]
    return merge(base, n_parts, w_parts, n_order, w_order, rank)


def solution(mesh):
    return jax.shard_map(
        functools.partial(on_device, mesh.shape["shard"], mesh.shape["group"]),
        mesh=mesh,
        in_specs=(
            P("parts", None, "shard", None),
            P("parts", None, ("shard", "group"), None),
            P("parts", None, None, ("shard", "group")),
            P("parts"),
        ),
        out_specs=P("parts", None, "shard", None),
        check_vma=False,
    )
```

```python
import functools

import jax
import jax.numpy as jnp
from jax import lax
from jax.experimental import pallas as pl
from jax.experimental.pallas import tpu as pltpu
from jax.sharding import PartitionSpec as P

adapter_scale = 0.5
out_slots = 4


def select_kernel(index_ref, narrow_ref, wide_ref, n_out, w_out, index, n_buf, w_buf, index_sem, sems):
    experts = index_ref.shape[0]
    rank = narrow_ref.shape[2]
    index_copy = pltpu.make_async_copy(index_ref, index, index_sem)
    index_copy.start()
    index_copy.wait()
    copies = []
    for e in range(experts):
        i = index[e]
        rows = pl.ds(e * rank, rank)
        copies.append(pltpu.make_async_copy(narrow_ref.at[i], n_buf.at[:, rows], sems.at[e, 0]))
        copies.append(pltpu.make_async_copy(wide_ref.at[i], w_buf.at[:, rows], sems.at[e, 1]))
    for copy in copies:
        copy.start()
    for copy in copies:
        copy.wait()
    for p in range(n_buf.shape[0]):
        n = n_buf[p].astype(jnp.float32) * adapter_scale
        n_out[p] = n.T.astype(n_out.dtype)
        w = w_buf[p].astype(jnp.float32).T.astype(w_out.dtype)
        for k in range(w_out.shape[0]):
            w_out[k, p] = w


def select(narrow, wide, index, copies):
    experts = index.shape[0]
    _, projections, rank, rows = narrow.shape
    columns = wide.shape[3]
    deep = experts * rank
    return pl.pallas_call(
        select_kernel,
        out_shape=(
            jax.ShapeDtypeStruct((projections, rows, deep), narrow.dtype),
            jax.ShapeDtypeStruct((copies, projections, columns, deep), wide.dtype),
        ),
        in_specs=[pl.BlockSpec(memory_space=pltpu.HBM)] * 3,
        out_specs=[pl.BlockSpec(memory_space=pltpu.VMEM)] * 2,
        scratch_shapes=[
            pltpu.SMEM((experts,), index.dtype),
            pltpu.VMEM((projections, deep, rows), narrow.dtype),
            pltpu.VMEM((projections, deep, columns), wide.dtype),
            pltpu.SemaphoreType.DMA,
            pltpu.SemaphoreType.DMA((experts, 2)),
        ],
        compiler_params=pltpu.CompilerParams(vmem_limit_bytes=4 * 2**20),
        name="select",
    )(*[pltpu.with_memory_space_constraint(x, pltpu.HBM) for x in (index, narrow, wide)])


def load_kernel(base_ref, out_ref, sem):
    copy = pltpu.make_async_copy(base_ref, out_ref, sem)
    copy.start()
    copy.wait()


def load(base):
    return pl.pallas_call(
        load_kernel,
        out_shape=jax.ShapeDtypeStruct(base.shape, base.dtype),
        in_specs=[pl.BlockSpec(memory_space=pltpu.HBM)],
        out_specs=pl.BlockSpec(memory_space=pltpu.VMEM),
        scratch_shapes=[pltpu.SemaphoreType.DMA],
        compiler_params=pltpu.CompilerParams(vmem_limit_bytes=24 * 2**20),
        cost_estimate=pl.CostEstimate(flops=0, bytes_accessed=2 * base.size, transcendentals=0),
        name="load",
    )(base)


def merge_kernel(n_order, w_order, rank, *refs):
    base_ref = refs[0]
    n_refs = refs[1 : 1 + len(n_order)]
    w_refs = refs[1 + len(n_order) : 1 + len(n_order) + len(w_order)]
    out_ref, w_all, out_buf, sems = refs[1 + len(n_order) + len(w_order) :]
    experts, projections = base_ref.shape[:2]
    rows = n_refs[0].shape[1]
    pieces, _, columns, _ = w_refs[0].shape
    wide_columns = base_ref.shape[3]
    step_columns = 256 if wide_columns % 256 == 0 else wide_columns
    g = lax.axis_index("group")

    for w_ref, place in zip(w_refs, w_order):
        for k in range(pieces):
            at = pl.multiple_of(place(k, g) * columns, columns)
            for p in range(projections):
                w_all[p, pl.ds(at, columns), :] = w_ref[k, p]

    lane_expert = lax.broadcasted_iota(jnp.int32, (rows, n_refs[0].shape[2]), 1) // rank
    step = 0
    copies = []
    for p in range(projections):
        for n_ref, place in zip(n_refs, n_order):
            at = pl.multiple_of(place(g) * rows, rows)
            for e in range(experts):
                slot = step % out_slots
                if step >= out_slots:
                    copies[step - out_slots].wait()
                n = n_ref[p]
                n = jnp.where(lane_expert == e, n, jnp.zeros_like(n))
                for f in range(0, wide_columns, step_columns):
                    delta = lax.dot_general(
                        n,
                        w_all[p, f : f + step_columns],
                        (((1,), (1,)), ((), ())),
                        preferred_element_type=jnp.float32,
                    )
                    b = base_ref[e, p, pl.ds(at, rows), f : f + step_columns]
                    out_buf[slot, :, f : f + step_columns] = (b.astype(jnp.float32) + delta).astype(out_buf.dtype)
                copy = pltpu.make_async_copy(out_buf.at[slot], out_ref.at[e, p, pl.ds(at, rows)], sems.at[slot])
                copy.start()
                copies.append(copy)
                step += 1
    for copy in copies[max(0, step - out_slots) :]:
        copy.wait()


def merge(base, n_parts, w_parts, n_order, w_order, rank):
    experts, projections, width, wide_columns = base.shape
    _, rows, deep = n_parts[0].shape
    in_vmem = pl.BlockSpec(memory_space=pltpu.VMEM)
    return pl.pallas_call(
        functools.partial(merge_kernel, n_order, w_order, rank),
        out_shape=jax.ShapeDtypeStruct(base.shape, base.dtype),
        in_specs=[in_vmem] * (1 + len(n_parts) + len(w_parts)),
        out_specs=pl.BlockSpec(memory_space=pl.ANY),
        scratch_shapes=[
            pltpu.VMEM((projections, wide_columns, deep), base.dtype),
            pltpu.VMEM((out_slots, rows, wide_columns), base.dtype),
            pltpu.SemaphoreType.DMA((out_slots,)),
        ],
        compiler_params=pltpu.CompilerParams(vmem_limit_bytes=30 * 2**20),
        cost_estimate=pl.CostEstimate(
            flops=2 * base.size * rank, bytes_accessed=4 * base.size, transcendentals=0
        ),
        name="merge",
    )(base, *n_parts, *w_parts)


def on_device(shards, groups, base, narrow, wide, adapted_expert_index):
    rank = narrow.shape[3]
    by_hand = groups == 4
    n, w = select(jnp.swapaxes(narrow, 2, 3), wide, adapted_expert_index, shards if by_hand else 1)
    axes = ("shard", "group")

    def flip(x, bit):
        pairs = [(g, g ^ bit) for g in range(groups)]
        return lax.ppermute(x, "group", pairs)

    if by_hand:
        n_x = flip(n, 2)
        w_line = lax.all_to_all(w, "shard", 0, 0)
        w_x = flip(w_line, 2)
        n_parts = [n, n_x, flip(n, 1), flip(n_x, 1)]
        w_parts = [w_line, w_x, flip(w_line, 1), flip(w_x, 1)]
        n_order = [lambda g, m=m: g ^ m for m in (0, 2, 1, 3)]
        w_order = [lambda k, g, m=m: k * groups + (g ^ m) for m in (0, 2, 1, 3)]
    else:
        n_parts = [lax.all_gather(n, "group", axis=1, tiled=True)]
        w_parts = [lax.all_gather(w, axes, axis=2, tiled=True)]
        n_order = [lambda g: 0]
        w_order = [lambda k, g: 0]
    return merge(load(base), n_parts, w_parts, n_order, w_order, rank)


def solution(mesh):
    return jax.shard_map(
        functools.partial(on_device, mesh.shape["shard"], mesh.shape["group"]),
        mesh=mesh,
        in_specs=(
            P("parts", None, "shard", None),
            P("parts", None, ("shard", "group"), None),
            P("parts", None, None, ("shard", "group")),
            P("parts"),
        ),
        out_specs=P("parts", None, "shard", None),
        check_vma=False,
    )
```

```python
import functools

import jax
import jax.numpy as jnp
from jax import lax
from jax.experimental import pallas as pl
from jax.experimental.pallas import tpu as pltpu
from jax.sharding import PartitionSpec as P

adapter_scale = 0.5
out_slots = 3
in_vmem = pl.BlockSpec(memory_space=pltpu.VMEM)
in_hbm = pl.BlockSpec(memory_space=pltpu.HBM)
anywhere = pl.BlockSpec(memory_space=pl.ANY)
mib = 2**20


def select_kernel(index_ref, narrow_ref, wide_ref, both_out, w_out, index, n_buf, w_buf, index_sem, sems):
    experts = index_ref.shape[0]
    rank = narrow_ref.shape[2]
    rows = n_buf.shape[2]
    index_copy = pltpu.make_async_copy(index_ref, index, index_sem)
    index_copy.start()
    index_copy.wait()
    n_copies, w_copies = [], []
    for e in range(experts):
        i = index[e]
        ranks = pl.ds(e * rank, rank)
        w_copies.append(pltpu.make_async_copy(wide_ref.at[i], w_buf.at[:, ranks], sems.at[e, 1]))
        n_copies.append(pltpu.make_async_copy(narrow_ref.at[i], n_buf.at[:, ranks], sems.at[e, 0]))
    for copy in w_copies + n_copies:
        copy.start()
    for copy in w_copies:
        copy.wait()
    for p in range(w_buf.shape[0]):
        w = w_buf[p].astype(jnp.float32).T.astype(w_out.dtype)
        w_out[p] = w
        both_out[p, rows:] = w
    for copy in n_copies:
        copy.wait()
    for p in range(n_buf.shape[0]):
        n = n_buf[p].astype(jnp.float32) * adapter_scale
        both_out[p, :rows] = n.T.astype(both_out.dtype)


def select(narrow, wide, index):
    experts = index.shape[0]
    _, projections, rank, rows = narrow.shape
    columns = wide.shape[3]
    deep = experts * rank
    return pl.pallas_call(
        select_kernel,
        out_shape=(
            jax.ShapeDtypeStruct((projections, rows + columns, deep), narrow.dtype),
            jax.ShapeDtypeStruct((projections, columns, deep), wide.dtype),
        ),
        in_specs=[in_hbm] * 3,
        out_specs=[in_vmem] * 2,
        scratch_shapes=[
            pltpu.SMEM((experts,), index.dtype),
            pltpu.VMEM((projections, deep, rows), narrow.dtype),
            pltpu.VMEM((projections, deep, columns), wide.dtype),
            pltpu.SemaphoreType.DMA,
            pltpu.SemaphoreType.DMA((experts, 2)),
        ],
        compiler_params=pltpu.CompilerParams(vmem_limit_bytes=4 * mib),
        name="select",
    )(*[pltpu.with_memory_space_constraint(x, pltpu.HBM) for x in (index, narrow, wide)])


def load_kernel(base_ref, out_ref, sem):
    copy = pltpu.make_async_copy(base_ref, out_ref, sem)
    copy.start()
    copy.wait()


def load(base):
    return pl.pallas_call(
        load_kernel,
        out_shape=jax.ShapeDtypeStruct(base.shape, base.dtype),
        in_specs=[in_hbm],
        out_specs=in_vmem,
        scratch_shapes=[pltpu.SemaphoreType.DMA],
        compiler_params=pltpu.CompilerParams(vmem_limit_bytes=32 * mib),
        cost_estimate=pl.CostEstimate(flops=0, bytes_accessed=2 * base.size, transcendentals=0),
        name="load",
    )(base)


def pack_kernel(*refs):
    out_ref = refs[-1]
    for k in range(out_ref.shape[0]):
        out_ref[k] = refs[k][...]


def pack(blocks, after):
    block = blocks[0]
    return pl.pallas_call(
        pack_kernel,
        out_shape=jax.ShapeDtypeStruct((len(blocks),) + block.shape, block.dtype),
        in_specs=[in_vmem] * len(blocks) + [anywhere],
        out_specs=in_vmem,
        compiler_params=pltpu.CompilerParams(vmem_limit_bytes=4 * mib),
        name="pack",
    )(*blocks, after)


def merge_kernel(rank, n_pieces, w_pieces, base_ref, *refs):
    out_ref, n_all, w_rows, w_all, out_buf, sems = refs[-6:]
    experts, projections, width, wide_columns = base_ref.shape
    deep = n_all.shape[2]
    f_step = 256 if wide_columns % 256 == 0 else wide_columns
    m_step = 512 if width % 512 == 0 else width
    halves = width // m_step
    tiles = experts * halves
    s, g = lax.axis_index("shard"), lax.axis_index("group")
    lane_expert = lax.broadcasted_iota(jnp.int32, (m_step, deep), 1) // rank

    def out_copy(p, t):
        step = p * tiles + t
        rows = pl.ds(pl.multiple_of((t % halves) * m_step, m_step), m_step)
        slot = lax.rem(step, out_slots)
        return pltpu.make_async_copy(out_buf.at[slot], out_ref.at[t // halves, p, rows], sems.at[slot])

    for p in range(projections):
        for i, pick, first, count, place in n_pieces:
            at = pl.multiple_of(place(s, g) * count, count)
            n_all[p, pl.ds(at, count), :] = refs[i][pick + (p, pl.ds(first, count))]
        for i, pick, first, count, place in w_pieces:
            at = pl.multiple_of(place(s, g) * count, count)
            w_rows[p, pl.ds(at, count), :] = refs[i][pick + (p, pl.ds(first, count))]
        for f in range(0, wide_columns, f_step):
            w_all[p, :, f : f + f_step] = w_rows[p, f : f + f_step].T

        def tile(t, _):
            step = p * tiles + t
            e = t // halves
            rows = pl.ds(pl.multiple_of((t % halves) * m_step, m_step), m_step)
            slot = lax.rem(step, out_slots)

            @pl.when(step >= out_slots)
            def _():
                out_copy(p, t).wait()

            n = n_all[p, rows, :]
            n = jnp.where(lane_expert == e, n, jnp.zeros_like(n))
            for f in range(0, wide_columns, f_step):
                delta = jnp.dot(n, w_all[p, :, f : f + f_step], preferred_element_type=jnp.float32)
                b = base_ref[e, p, rows, f : f + f_step].astype(jnp.float32)
                out_buf[slot, :, f : f + f_step] = (b + delta).astype(out_buf.dtype)
            out_copy(p, t).start()
            return 0

        lax.fori_loop(0, tiles, tile, 0)
    for step in range(max(0, projections * tiles - out_slots), projections * tiles):
        out_copy(step // tiles, step % tiles).wait()


def merge(base, parts, n_pieces, w_pieces, rank):
    experts, projections, width, wide_columns = base.shape
    deep = parts[0].shape[-1]
    m_step = 512 if width % 512 == 0 else width
    return pl.pallas_call(
        functools.partial(merge_kernel, rank, n_pieces, w_pieces),
        out_shape=jax.ShapeDtypeStruct(base.shape, base.dtype),
        in_specs=[in_vmem] * (1 + len(parts)),
        out_specs=anywhere,
        scratch_shapes=[
            pltpu.VMEM((projections, width, deep), base.dtype),
            pltpu.VMEM((projections, wide_columns, deep), base.dtype),
            pltpu.VMEM((projections, deep, wide_columns), base.dtype),
            pltpu.VMEM((out_slots, m_step, wide_columns), base.dtype),
            pltpu.SemaphoreType.DMA((out_slots,)),
        ],
        compiler_params=pltpu.CompilerParams(vmem_limit_bytes=32 * mib),
        cost_estimate=pl.CostEstimate(
            flops=2 * base.size * rank, bytes_accessed=4 * base.size, transcendentals=0
        ),
        name="merge",
    )(base, *parts)


def on_device(shards, groups, base, narrow, wide, adapted_expert_index):
    rank = narrow.shape[3]
    rows, columns = narrow.shape[2], wide.shape[3]
    both, w = select(jnp.swapaxes(narrow, 2, 3), wide, adapted_expert_index)
    base = load(base)
    axes = ("shard", "group")

    if shards != 4 or groups != 4:
        n = lax.all_gather(both[:, :rows], "group", axis=1, tiled=True)
        w = lax.all_gather(w, axes, axis=1, tiled=True)
        whole = lambda s, g: 0
        n_pieces = [(0, (), 0, rows * groups, whole)]
        w_pieces = [(1, (), 0, columns * shards * groups, whole)]
        return merge(base, [n, w], n_pieces, w_pieces, rank)

    def swap(x, axis, bit):
        return lax.ppermute(x, axis, [(i, i ^ bit) for i in range(4)])

    line = pack([swap(w, "shard", k) for k in (1, 2, 3)], base)
    both_x = swap(both, "group", 2)
    line_x = swap(line, "group", 2)
    parts = [both, both_x, line, line_x]
    parts += [swap(x, "group", 1) for x in parts]
    n_pieces, w_pieces = [], []
    for i, m in ((0, 0), (1, 2), (4, 1), (5, 3)):
        n_pieces.append((i, (), 0, rows, lambda s, g, m=m: g ^ m))
        w_pieces.append((i, (), rows, columns, lambda s, g, m=m: s * groups + (g ^ m)))
        for k in (1, 2, 3):
            w_pieces.append((i + 2, (k - 1,), 0, columns, lambda s, g, m=m, k=k: (s ^ k) * groups + (g ^ m)))
    return merge(base, parts, n_pieces, w_pieces, rank)


def solution(mesh):
    return jax.shard_map(
        functools.partial(on_device, mesh.shape["shard"], mesh.shape["group"]),
        mesh=mesh,
        in_specs=(
            P("parts", None, "shard", None),
            P("parts", None, ("shard", "group"), None),
            P("parts", None, None, ("shard", "group")),
            P("parts"),
        ),
        out_specs=P("parts", None, "shard", None),
        check_vma=False,
    )
```

```python
import functools
import typing

import jax
import jax.numpy as jnp
from jax import lax
from jax.experimental import pallas as pl
from jax.experimental.pallas import tpu as pltpu
from jax.sharding import PartitionSpec as P

adapter_scale = 0.5
out_slots = 6
tile_rows = 256
in_vmem = pl.BlockSpec(memory_space=pltpu.VMEM)
in_hbm = pl.BlockSpec(memory_space=pltpu.HBM)
anywhere = pl.BlockSpec(memory_space=pl.ANY)
vmem_limit = 24 * 2**20


def select_kernel(index_ref, narrow_ref, wide_ref, both_out, w_out, index, n_buf, w_buf, index_sem, sems):
    experts = index_ref.shape[0]
    rank = narrow_ref.shape[2]
    rows = n_buf.shape[2]
    index_copy = pltpu.make_async_copy(index_ref, index, index_sem)
    index_copy.start()
    index_copy.wait()
    n_copies, w_copies = [], []
    for e in range(experts):
        i = index[e]
        ranks = pl.ds(e * rank, rank)
        w_copies.append(pltpu.make_async_copy(wide_ref.at[i], w_buf.at[:, ranks], sems.at[e, 1]))
        n_copies.append(pltpu.make_async_copy(narrow_ref.at[i], n_buf.at[:, ranks], sems.at[e, 0]))
    for copy in w_copies + n_copies:
        copy.start()
    for copy in w_copies:
        copy.wait()
    for p in range(w_buf.shape[0]):
        w = w_buf[p].astype(jnp.float32).T.astype(w_out.dtype)
        w_out[p] = w
        both_out[p, rows:] = w
    for copy in n_copies:
        copy.wait()
    for p in range(n_buf.shape[0]):
        n = n_buf[p].astype(jnp.float32) * adapter_scale
        both_out[p, :rows] = n.T.astype(both_out.dtype)


def select(narrow, wide, index):
    experts = index.shape[0]
    _, projections, rank, rows = narrow.shape
    columns = wide.shape[3]
    deep = experts * rank
    return pl.pallas_call(
        select_kernel,
        out_shape=(
            jax.ShapeDtypeStruct((projections, rows + columns, deep), narrow.dtype),
            jax.ShapeDtypeStruct((projections, columns, deep), wide.dtype),
        ),
        in_specs=[in_hbm] * 3,
        out_specs=[in_vmem] * 2,
        scratch_shapes=[
            pltpu.SMEM((experts,), index.dtype),
            pltpu.VMEM((projections, deep, rows), narrow.dtype),
            pltpu.VMEM((projections, deep, columns), wide.dtype),
            pltpu.SemaphoreType.DMA,
            pltpu.SemaphoreType.DMA((experts, 2)),
        ],
        compiler_params=pltpu.CompilerParams(vmem_limit_bytes=vmem_limit),
        name="select",
    )(*[pltpu.with_memory_space_constraint(x, pltpu.HBM) for x in (index, narrow, wide)])


def pack_kernel(count, *refs):
    out_ref = refs[-1]
    at = 0
    for ref in refs[:count]:
        rows = ref.shape[1]
        out_ref[:, at : at + rows] = ref[...]
        at += rows


def pack(blocks, after=()):
    projections, _, deep = blocks[0].shape
    rows = sum(x.shape[1] for x in blocks)
    return pl.pallas_call(
        functools.partial(pack_kernel, len(blocks)),
        out_shape=jax.ShapeDtypeStruct((projections, rows, deep), blocks[0].dtype),
        in_specs=[in_vmem] * len(blocks) + [anywhere] * len(after),
        out_specs=in_vmem,
        compiler_params=pltpu.CompilerParams(vmem_limit_bytes=vmem_limit),
        name="pack",
    )(*blocks, *after)


def merge_kernel(plan, count, base_ref, *refs):
    out_ref, token, n_all, w_rows, w_all, out_buf, sems = refs[-7:]
    experts, _, width, _ = base_ref.shape
    deep, span = w_all.shape
    m_step = out_buf.shape[1]
    f_step = 256 if span % 256 == 0 else span
    strips = width // m_step
    tiles = experts * strips
    s, g = lax.axis_index("shard"), lax.axis_index("group")
    lane_expert = lax.broadcasted_iota(jnp.int32, (m_step, deep), 1) // plan.rank
    first_column = pl.multiple_of(plan.chunk(s) * span, span)

    def out_copy(p, step):
        t = lax.rem(step, tiles)
        rows = pl.ds(pl.multiple_of((t % strips) * m_step, m_step), m_step)
        slot = lax.rem(step, out_slots)
        place = out_ref.at[t // strips, p, rows, pl.ds(first_column, span)]
        return pltpu.make_async_copy(out_buf.at[slot], place, sems.at[slot])

    for done, p in enumerate(plan.projections):
        for i, first, rows, place in plan.n_pieces:
            at = pl.multiple_of(place(s, g) * rows, rows)
            n_all[pl.ds(at, rows), :] = refs[i][p, pl.ds(first, rows)]
        for i, first, rows, place in plan.w_pieces:
            at = pl.multiple_of(place(s, g) * rows, rows)
            w_rows[pl.ds(at, rows), :] = refs[i][p, pl.ds(first, rows)]
        for f in range(0, span, f_step):
            w_all[:, f : f + f_step] = w_rows[f : f + f_step].T

        def tile(step, _):
            t = lax.rem(step, tiles)
            e = t // strips
            rows = pl.ds(pl.multiple_of((t % strips) * m_step, m_step), m_step)
            slot = lax.rem(step, out_slots)

            @pl.when(step >= out_slots)
            def _():
                out_copy(p, step).wait()

            n = n_all[rows, :]
            n = jnp.where(lane_expert == e, n, jnp.zeros_like(n))
            for f in range(0, span, f_step):
                delta = jnp.dot(n, w_all[:, f : f + f_step], preferred_element_type=jnp.float32)
                b = base_ref[e, p, rows, pl.ds(first_column + f, f_step)].astype(jnp.float32)
                out_buf[slot, :, f : f + f_step] = (b + delta).astype(out_buf.dtype)
            out_copy(p, step).start()
            return 0

        lax.fori_loop(done * tiles, (done + 1) * tiles, tile, 0)
    steps = len(plan.projections) * tiles
    for step in range(max(0, steps - out_slots), steps):
        out_copy(plan.projections[-1], step).wait()
    token[...] = jnp.zeros_like(token)


class Plan(typing.NamedTuple):
    rank: int
    projections: tuple
    span: int
    chunk: typing.Callable
    n_pieces: list
    w_pieces: list


def merge(plan, base, parts, out=None, after=()):
    experts, projections, width, _ = base.shape
    deep = parts[0].shape[-1]
    m_step = tile_rows if width % tile_rows == 0 else width
    operands = [base, *parts, *after] + ([] if out is None else [out])
    share = len(plan.projections) * plan.span * experts * width
    return pl.pallas_call(
        functools.partial(merge_kernel, plan, len(parts)),
        out_shape=(jax.ShapeDtypeStruct(base.shape, base.dtype), jax.ShapeDtypeStruct((8, 128), jnp.float32)),
        in_specs=[in_vmem] * (1 + len(parts)) + [anywhere] * (len(operands) - 1 - len(parts)),
        out_specs=(in_hbm, in_vmem),
        scratch_shapes=[
            pltpu.VMEM((width, deep), base.dtype),
            pltpu.VMEM((plan.span, deep), base.dtype),
            pltpu.VMEM((deep, plan.span), base.dtype),
            pltpu.VMEM((out_slots, m_step, plan.span), base.dtype),
            pltpu.SemaphoreType.DMA((out_slots,)),
        ],
        input_output_aliases={} if out is None else {len(operands) - 1: 0},
        compiler_params=pltpu.CompilerParams(vmem_limit_bytes=vmem_limit),
        cost_estimate=pl.CostEstimate(flops=2 * share * plan.rank, bytes_accessed=4 * share, transcendentals=0),
        name="merge",
    )(*operands)


def on_device(shards, groups, base, narrow, wide, adapted_expert_index):
    rank = narrow.shape[3]
    rows, columns = narrow.shape[2], wide.shape[3]
    projections = tuple(range(base.shape[1]))
    both, w = select(jnp.swapaxes(narrow, 2, 3), wide, adapted_expert_index)
    axes = ("shard", "group")

    if shards != 4 or groups != 4:
        n = lax.all_gather(both[:, :rows], "group", axis=1, tiled=True)
        w = lax.all_gather(w, axes, axis=1, tiled=True)
        whole = lambda s, g: 0
        plan = Plan(
            rank,
            projections,
            columns * shards * groups,
            lambda s: 0,
            [(0, 0, rows * groups, whole)],
            [(1, 0, columns * shards * groups, whole)],
        )
        return merge(plan, base, [n, w])[0]

    def swap(x, axis, bit):
        return lax.ppermute(x, axis, [(i, i ^ bit) for i in range(4)])

    base = swap(base, "group", 0)
    w3, w2, w1 = [swap(w, "shard", k) for k in (3, 2, 1)]
    line = pack([w2, w3])
    own_a = pack([both, swap(both, "group", 2), w1, swap(w1, "group", 2)], (line,))
    other_a = swap(own_a, "group", 1)
    line_x = swap(line, "group", 2)
    half = rows + columns
    n_pieces = [
        (i, first, rows, lambda s, g, m=m: g ^ m)
        for i, first, m in ((0, 0, 0), (0, half, 2), (1, 0, 1), (1, half, 3))
    ]

    def w_piece(i, first, k, m):
        return (i, first, columns, lambda s, g: ((s ^ k) % 2) * groups + (g ^ m))

    near, far = [], []
    for i, m in ((0, 0), (1, 1)):
        near += [w_piece(i, rows, 0, m), w_piece(i, half + rows, 0, m ^ 2)]
        near += [w_piece(i, 2 * half, 1, m), w_piece(i, 2 * half + columns, 1, m ^ 2)]
        for at, k in ((0, 2), (1, 3)):
            far += [w_piece(i + 2, at * columns, k, m), w_piece(i + 2, (at + 2) * columns, k, m ^ 2)]
    span = 2 * columns * groups
    near_plan = Plan(rank, projections, span, lambda s: s // 2, n_pieces, near)
    far_plan = Plan(rank, projections, span, lambda s: 1 - s // 2, n_pieces, far)
    parts = [own_a, other_a]
    out, token = merge(near_plan._replace(projections=projections[:2]), base, parts, after=(line,))
    own_b = pack([line, line_x], (token,))
    other_b = swap(own_b, "group", 1)
    out, _ = merge(near_plan._replace(projections=projections[2:]), base, parts, out, after=(own_b,))
    return merge(far_plan, base, parts + [own_b, other_b], out)[0]


def solution(mesh):
    return jax.shard_map(
        functools.partial(on_device, mesh.shape["shard"], mesh.shape["group"]),
        mesh=mesh,
        in_specs=(
            P("parts", None, "shard", None),
            P("parts", None, ("shard", "group"), None),
            P("parts", None, None, ("shard", "group")),
            P("parts"),
        ),
        out_specs=P("parts", None, "shard", None),
        check_vma=False,
    )
```

```python
import functools
import math
import typing

import jax
import jax.numpy as jnp
from jax import lax
from jax.experimental import pallas as pl
from jax.experimental.pallas import tpu as pltpu
from jax.sharding import PartitionSpec as P

adapter_scale = 0.5
out_slots = 3
tile_rows = 512
in_vmem = pl.BlockSpec(memory_space=pltpu.VMEM)
in_hbm = pl.BlockSpec(memory_space=pltpu.HBM)
anywhere = pl.BlockSpec(memory_space=pl.ANY)
vmem_limit = 24 * 2**20


def select_kernel(index_ref, narrow_ref, wide_ref, both_out, w_out, index, n_buf, w_buf, index_sem, sems):
    experts = index_ref.shape[0]
    rank = narrow_ref.shape[2]
    rows = n_buf.shape[2]
    index_copy = pltpu.make_async_copy(index_ref, index, index_sem)
    index_copy.start()
    index_copy.wait()
    n_copies, w_copies = [], []
    for e in range(experts):
        i = index[e]
        ranks = pl.ds(e * rank, rank)
        w_copies.append(pltpu.make_async_copy(wide_ref.at[i], w_buf.at[:, ranks], sems.at[e, 1]))
        n_copies.append(pltpu.make_async_copy(narrow_ref.at[i], n_buf.at[:, ranks], sems.at[e, 0]))
    for copy in w_copies + n_copies:
        copy.start()
    for copy in w_copies:
        copy.wait()
    for p in range(w_buf.shape[0]):
        w = w_buf[p].astype(jnp.float32).T.astype(w_out.dtype)
        w_out[p] = w
        both_out[p, rows:] = w
    for copy in n_copies:
        copy.wait()
    for p in range(n_buf.shape[0]):
        n = n_buf[p].astype(jnp.float32) * adapter_scale
        both_out[p, :rows] = n.T.astype(both_out.dtype)


def select(narrow, wide, index):
    experts = index.shape[0]
    _, projections, rank, rows = narrow.shape
    columns = wide.shape[3]
    deep = experts * rank
    return pl.pallas_call(
        select_kernel,
        out_shape=(
            jax.ShapeDtypeStruct((projections, rows + columns, deep), narrow.dtype),
            jax.ShapeDtypeStruct((projections, columns, deep), wide.dtype),
        ),
        in_specs=[in_hbm] * 3,
        out_specs=[in_vmem] * 2,
        scratch_shapes=[
            pltpu.SMEM((experts,), index.dtype),
            pltpu.VMEM((projections, deep, rows), narrow.dtype),
            pltpu.VMEM((projections, deep, columns), wide.dtype),
            pltpu.SemaphoreType.DMA,
            pltpu.SemaphoreType.DMA((experts, 2)),
        ],
        compiler_params=pltpu.CompilerParams(vmem_limit_bytes=vmem_limit),
        name="select",
    )(*[pltpu.with_memory_space_constraint(x, pltpu.HBM) for x in (index, narrow, wide)])


def load_kernel(loaded, base_ref, _, out_ref, sem):
    copy = pltpu.make_async_copy(base_ref.at[:, pl.ds(0, loaded)], out_ref, sem)
    copy.start()
    copy.wait()


def load(base, loaded, after):
    shape = base.shape[:1] + (loaded,) + base.shape[2:]
    return pl.pallas_call(
        functools.partial(load_kernel, loaded),
        out_shape=jax.ShapeDtypeStruct(shape, base.dtype),
        in_specs=[in_hbm, anywhere],
        out_specs=in_vmem,
        scratch_shapes=[pltpu.SemaphoreType.DMA],
        compiler_params=pltpu.CompilerParams(vmem_limit_bytes=vmem_limit),
        cost_estimate=pl.CostEstimate(flops=0, bytes_accessed=2 * math.prod(shape), transcendentals=0),
        name="load",
    )(base, after)


def pack_kernel(count, *refs):
    out_ref = refs[-1]
    at = 0
    for ref in refs[:count]:
        rows = ref.shape[1]
        out_ref[:, at : at + rows] = ref[...]
        at += rows


def pack(blocks, after=()):
    projections, _, deep = blocks[0].shape
    rows = sum(x.shape[1] for x in blocks)
    return pl.pallas_call(
        functools.partial(pack_kernel, len(blocks)),
        out_shape=jax.ShapeDtypeStruct((projections, rows, deep), blocks[0].dtype),
        in_specs=[in_vmem] * len(blocks) + [anywhere] * len(after),
        out_specs=in_vmem,
        compiler_params=pltpu.CompilerParams(vmem_limit_bytes=vmem_limit),
        name="pack",
    )(*blocks, *after)


def merge_kernel(plan, has_loaded, base_ref, *refs):
    if has_loaded:
        loaded_ref, refs = refs[0], refs[1:]
        loaded = loaded_ref.shape[1]
    else:
        loaded = 0
    out_ref, token, n_all, w_rows, w_all, out_buf, sems, late_buf, late_sems = refs[-9:]
    experts, _, width, _ = base_ref.shape
    deep, span = w_all.shape
    m_step = out_buf.shape[1]
    f_step = 256 if span % 256 == 0 else span
    strips = width // m_step
    tiles = experts * strips
    s, g = lax.axis_index("shard"), lax.axis_index("group")
    lane_expert = lax.broadcasted_iota(jnp.int32, (m_step, deep), 1) // plan.rank
    late = [p for p in plan.projections if p >= loaded]

    def merge_chunk(first_column):
        columns = pl.ds(first_column, span)

        def late_copy(p):
            at = p - late[0]
            return pltpu.make_async_copy(base_ref.at[:, p, :, columns], late_buf.at[at], late_sems.at[at])

        def out_copy(p, step):
            t = lax.rem(step, tiles)
            rows = pl.ds(pl.multiple_of((t % strips) * m_step, m_step), m_step)
            slot = lax.rem(step, out_slots)
            return pltpu.make_async_copy(out_buf.at[slot], out_ref.at[t // strips, p, rows, columns], sems.at[slot])

        for p in late:
            late_copy(p).start()
        for done, p in enumerate(plan.projections):
            for i, first, rows, place in plan.n_pieces:
                at = pl.multiple_of(place(s, g) * rows, rows)
                n_all[pl.ds(at, rows), :] = refs[i][p, pl.ds(first, rows)]
            for i, first, rows, place in plan.w_pieces:
                at = pl.multiple_of(place(s, g) * rows, rows)
                w_rows[pl.ds(at, rows), :] = refs[i][p, pl.ds(first, rows)]
            for f in range(0, span, f_step):
                w_all[:, f : f + f_step] = w_rows[f : f + f_step].T
            if p in late:
                late_copy(p).wait()

            def tile(step, _):
                t = lax.rem(step, tiles)
                e = t // strips
                rows = pl.ds(pl.multiple_of((t % strips) * m_step, m_step), m_step)
                slot = lax.rem(step, out_slots)

                @pl.when(step >= out_slots)
                def _():
                    out_copy(p, step).wait()

                n = n_all[rows, :]
                n = jnp.where(lane_expert == e, n, jnp.zeros_like(n))
                for f in range(0, span, f_step):
                    delta = jnp.dot(n, w_all[:, f : f + f_step], preferred_element_type=jnp.float32)
                    if p in late:
                        b = late_buf[p - late[0], e, rows, f : f + f_step]
                    else:
                        b = loaded_ref[e, p, rows, first_column + f : first_column + f + f_step]
                    out_buf[slot, :, f : f + f_step] = (b.astype(jnp.float32) + delta).astype(out_buf.dtype)
                out_copy(p, step).start()
                return 0

            lax.fori_loop(done * tiles, (done + 1) * tiles, tile, 0)
        steps = len(plan.projections) * tiles
        for step in range(max(0, steps - out_slots), steps):
            out_copy(plan.projections[-1], step).wait()

    for c in range(plan.chunks):
        pl.when(plan.chunk(s) == c)(functools.partial(merge_chunk, c * span))
    token[...] = jnp.zeros_like(token)


class Plan(typing.NamedTuple):
    rank: int
    projections: tuple
    span: int
    chunks: int
    chunk: typing.Callable
    n_pieces: list
    w_pieces: list


def merge(plan, base, parts, loaded=None, out=None, after=()):
    experts, _, width, _ = base.shape
    deep = parts[0].shape[-1]
    m_step = tile_rows if width % tile_rows == 0 else width
    share = len(plan.projections) * plan.span * experts * width
    in_place = [] if loaded is None else [loaded]
    late = len([p for p in plan.projections if loaded is None or p >= loaded.shape[1]])
    extra = [*after] + ([] if out is None else [out])
    operands = [pltpu.with_memory_space_constraint(base, pltpu.HBM), *in_place, *parts, *extra]
    return pl.pallas_call(
        functools.partial(merge_kernel, plan, loaded is not None),
        out_shape=(jax.ShapeDtypeStruct(base.shape, base.dtype), jax.ShapeDtypeStruct((8, 128), jnp.float32)),
        in_specs=[in_hbm] + [in_vmem] * len(in_place + parts) + [anywhere] * len(extra),
        out_specs=(in_hbm, in_vmem),
        scratch_shapes=[
            pltpu.VMEM((width, deep), base.dtype),
            pltpu.VMEM((plan.span, deep), base.dtype),
            pltpu.VMEM((deep, plan.span), base.dtype),
            pltpu.VMEM((out_slots, m_step, plan.span), base.dtype),
            pltpu.SemaphoreType.DMA((out_slots,)),
            pltpu.VMEM((max(late, 1), experts, width if late else 16, plan.span), base.dtype),
            pltpu.SemaphoreType.DMA((max(late, 1),)),
        ],
        input_output_aliases={} if out is None else {len(operands) - 1: 0},
        compiler_params=pltpu.CompilerParams(vmem_limit_bytes=vmem_limit),
        cost_estimate=pl.CostEstimate(flops=2 * share * plan.rank, bytes_accessed=4 * share, transcendentals=0),
        name="merge",
    )(*operands)


def on_device(shards, groups, base, narrow, wide, adapted_expert_index):
    rank = narrow.shape[3]
    rows, columns = narrow.shape[2], wide.shape[3]
    projections = tuple(range(base.shape[1]))
    both, w = select(jnp.swapaxes(narrow, 2, 3), wide, adapted_expert_index)
    axes = ("shard", "group")

    if shards != 4 or groups != 4:
        n = lax.all_gather(both[:, :rows], "group", axis=1, tiled=True)
        w = lax.all_gather(w, axes, axis=1, tiled=True)
        whole = lambda s, g: 0
        plan = Plan(
            rank,
            projections,
            columns * shards * groups,
            1,
            lambda s: 0,
            [(0, 0, rows * groups, whole)],
            [(1, 0, columns * shards * groups, whole)],
        )
        return merge(plan, base, [n, w])[0]

    def swap(x, axis, bit):
        return lax.ppermute(x, axis, [(i, i ^ bit) for i in range(4)])

    w1 = swap(w, "shard", 1)
    pair = pack([w, w1])
    line = swap(pair, "shard", 2)
    loaded = load(base, len(projections), pair)
    own_a = pack([both, swap(both, "group", 2), w1, swap(w1, "group", 2)], (loaded, line))
    other_a = swap(own_a, "group", 1)
    line_x = swap(line, "group", 2)
    half = rows + columns
    n_pieces = [
        (i, first, rows, lambda s, g, m=m: g ^ m)
        for i, first, m in ((0, 0, 0), (0, half, 2), (1, 0, 1), (1, half, 3))
    ]

    def w_piece(i, first, k, m):
        return (i, first, columns, lambda s, g: ((s ^ k) % 2) * groups + (g ^ m))

    near, far = [], []
    for i, m in ((0, 0), (1, 1)):
        near += [w_piece(i, rows, 0, m), w_piece(i, half + rows, 0, m ^ 2)]
        near += [w_piece(i, 2 * half, 1, m), w_piece(i, 2 * half + columns, 1, m ^ 2)]
        for at, k in ((0, 2), (1, 3)):
            far += [w_piece(i + 2, at * columns, k, m), w_piece(i + 2, (at + 2) * columns, k, m ^ 2)]
    span = 2 * columns * groups
    near_plan = Plan(rank, projections, span, 2, lambda s: s // 2, n_pieces, near)
    far_plan = Plan(rank, projections, span, 2, lambda s: 1 - s // 2, n_pieces, far)
    parts = [own_a, other_a]
    out, token = merge(near_plan._replace(projections=projections[:2]), base, parts, loaded, after=(line,))
    own_b = pack([line, line_x], (token,))
    other_b = swap(own_b, "group", 1)
    out, _ = merge(near_plan._replace(projections=projections[2:]), base, parts, loaded, out, after=(own_b,))
    return merge(far_plan, base, parts + [own_b, other_b], loaded, out)[0]


def solution(mesh):
    return jax.shard_map(
        functools.partial(on_device, mesh.shape["shard"], mesh.shape["group"]),
        mesh=mesh,
        in_specs=(
            P("parts", None, "shard", None),
            P("parts", None, ("shard", "group"), None),
            P("parts", None, None, ("shard", "group")),
            P("parts"),
        ),
        out_specs=P("parts", None, "shard", None),
        check_vma=False,
    )
```

```python
import functools
import typing

import jax
import jax.numpy as jnp
from jax import lax
from jax.experimental import pallas as pl
from jax.experimental.pallas import tpu as pltpu
from jax.sharding import PartitionSpec as P

adapter_scale = 0.5
out_slots = 4
tile_rows = 512
in_vmem = pl.BlockSpec(memory_space=pltpu.VMEM)
in_hbm = pl.BlockSpec(memory_space=pltpu.HBM)
anywhere = pl.BlockSpec(memory_space=pl.ANY)
vmem_limit = 24 * 2**20


def select_kernel(index_ref, narrow_ref, wide_ref, both_out, w_out, index, n_buf, w_buf, index_sem, sems):
    experts = index_ref.shape[0]
    rank = narrow_ref.shape[2]
    rows = n_buf.shape[2]
    index_copy = pltpu.make_async_copy(index_ref, index, index_sem)
    index_copy.start()
    index_copy.wait()
    n_copies, w_copies = [], []
    for e in range(experts):
        i = index[e]
        ranks = pl.ds(e * rank, rank)
        w_copies.append(pltpu.make_async_copy(wide_ref.at[i], w_buf.at[:, ranks], sems.at[e, 1]))
        n_copies.append(pltpu.make_async_copy(narrow_ref.at[i], n_buf.at[:, ranks], sems.at[e, 0]))
    for copy in w_copies + n_copies:
        copy.start()
    for copy in w_copies:
        copy.wait()
    for p in range(w_buf.shape[0]):
        w = w_buf[p].astype(jnp.float32).T.astype(w_out.dtype)
        w_out[p] = w
        both_out[p, rows:] = w
    for copy in n_copies:
        copy.wait()
    for p in range(n_buf.shape[0]):
        n = n_buf[p].astype(jnp.float32) * adapter_scale
        both_out[p, :rows] = n.T.astype(both_out.dtype)


def select(narrow, wide, index):
    experts = index.shape[0]
    _, projections, rank, rows = narrow.shape
    columns = wide.shape[3]
    deep = experts * rank
    return pl.pallas_call(
        select_kernel,
        out_shape=(
            jax.ShapeDtypeStruct((projections, rows + columns, deep), narrow.dtype),
            jax.ShapeDtypeStruct((projections, columns, deep), wide.dtype),
        ),
        in_specs=[in_hbm] * 3,
        out_specs=[in_vmem] * 2,
        scratch_shapes=[
            pltpu.SMEM((experts,), index.dtype),
            pltpu.VMEM((projections, deep, rows), narrow.dtype),
            pltpu.VMEM((projections, deep, columns), wide.dtype),
            pltpu.SemaphoreType.DMA,
            pltpu.SemaphoreType.DMA((experts, 2)),
        ],
        compiler_params=pltpu.CompilerParams(vmem_limit_bytes=vmem_limit),
        name="select",
    )(*[pltpu.with_memory_space_constraint(x, pltpu.HBM) for x in (index, narrow, wide)])


def load_kernel(base_ref, _, out_ref, sem):
    copy = pltpu.make_async_copy(base_ref, out_ref, sem)
    copy.start()
    copy.wait()


def load(base, after):
    return pl.pallas_call(
        load_kernel,
        out_shape=jax.ShapeDtypeStruct(base.shape, base.dtype),
        in_specs=[in_hbm, anywhere],
        out_specs=in_vmem,
        scratch_shapes=[pltpu.SemaphoreType.DMA],
        compiler_params=pltpu.CompilerParams(vmem_limit_bytes=vmem_limit),
        cost_estimate=pl.CostEstimate(flops=0, bytes_accessed=2 * base.size, transcendentals=0),
        name="load",
    )(base, after)


def pack_kernel(count, *refs):
    out_ref = refs[-1]
    at = 0
    for ref in refs[:count]:
        rows = ref.shape[1]
        out_ref[:, at : at + rows] = ref[...]
        at += rows


def pack(blocks, after=()):
    projections, _, deep = blocks[0].shape
    rows = sum(x.shape[1] for x in blocks)
    return pl.pallas_call(
        functools.partial(pack_kernel, len(blocks)),
        out_shape=jax.ShapeDtypeStruct((projections, rows, deep), blocks[0].dtype),
        in_specs=[in_vmem] * len(blocks) + [anywhere] * len(after),
        out_specs=in_vmem,
        compiler_params=pltpu.CompilerParams(vmem_limit_bytes=vmem_limit),
        name="pack",
    )(*blocks, *after)


def merge_kernel(plan, base_ref, *refs):
    out_ref, token, n_all, w_rows, w_all, out_buf, sems = refs[-7:]
    experts, projections, width, _ = base_ref.shape
    _, deep, span = w_all.shape
    m_step = out_buf.shape[1]
    f_step = 256 if span % 256 == 0 else span
    strips = width // m_step
    tiles = experts * strips
    steps = projections * tiles
    s, g = lax.axis_index("shard"), lax.axis_index("group")
    lane_expert = lax.broadcasted_iota(jnp.int32, (m_step, deep), 1) // plan.rank

    def prepare(p, _):
        for i, first, rows, place in plan.n_pieces:
            at = pl.multiple_of(place(s, g) * rows, rows)
            n_all[p, pl.ds(at, rows), :] = refs[i][p, pl.ds(first, rows)]
        for i, first, rows, place in plan.w_pieces:
            at = pl.multiple_of(place(s, g) * rows, rows)
            w_rows[pl.ds(at, rows), :] = refs[i][p, pl.ds(first, rows)]
        for f in range(0, span, f_step):
            w_all[p, :, f : f + f_step] = w_rows[f : f + f_step].T
        return 0

    lax.fori_loop(0, projections, prepare, 0)

    def merge_chunk(first_column):
        columns = pl.ds(first_column, span)

        def out_copy(step):
            p, t = step // tiles, lax.rem(step, tiles)
            rows = pl.ds(pl.multiple_of(lax.rem(t, strips) * m_step, m_step), m_step)
            slot = lax.rem(step, out_slots)
            return pltpu.make_async_copy(out_buf.at[slot], out_ref.at[t // strips, p, rows, columns], sems.at[slot])

        def tile(step, _):
            p, t = step // tiles, lax.rem(step, tiles)
            e = t // strips
            rows = pl.ds(pl.multiple_of(lax.rem(t, strips) * m_step, m_step), m_step)
            slot = lax.rem(step, out_slots)

            @pl.when(step >= out_slots)
            def _():
                out_copy(step - out_slots).wait()

            n = n_all[p, rows, :]
            n = jnp.where(lane_expert == e, n, jnp.zeros_like(n))
            for f in range(0, span, f_step):
                delta = jnp.dot(n, w_all[p, :, f : f + f_step], preferred_element_type=jnp.float32)
                b = base_ref[e, p, rows, first_column + f : first_column + f + f_step]
                out_buf[slot, :, f : f + f_step] = (b.astype(jnp.float32) + delta).astype(out_buf.dtype)
            out_copy(step).start()
            return 0

        lax.fori_loop(0, steps, tile, 0)
        for step in range(max(0, steps - out_slots), steps):
            out_copy(jnp.int32(step)).wait()

    for c in range(plan.chunks):
        pl.when(plan.chunk(s) == c)(functools.partial(merge_chunk, c * span))
    token[...] = jnp.zeros_like(token)


class Plan(typing.NamedTuple):
    rank: int
    span: int
    chunks: int
    chunk: typing.Callable
    n_pieces: list
    w_pieces: list


def merge(plan, base, parts, out=None, after=()):
    experts, projections, width, _ = base.shape
    deep = parts[0].shape[-1]
    m_step = tile_rows if width % tile_rows == 0 else width
    share = projections * plan.span * experts * width
    extra = [*after] + ([] if out is None else [out])
    operands = [base, *parts, *extra]
    return pl.pallas_call(
        functools.partial(merge_kernel, plan),
        out_shape=(jax.ShapeDtypeStruct(base.shape, base.dtype), jax.ShapeDtypeStruct((8, 128), jnp.float32)),
        in_specs=[in_vmem] * (1 + len(parts)) + [anywhere] * len(extra),
        out_specs=(in_hbm, in_vmem),
        scratch_shapes=[
            pltpu.VMEM((projections, width, deep), base.dtype),
            pltpu.VMEM((plan.span, deep), base.dtype),
            pltpu.VMEM((projections, deep, plan.span), base.dtype),
            pltpu.VMEM((out_slots, m_step, plan.span), base.dtype),
            pltpu.SemaphoreType.DMA((out_slots,)),
        ],
        input_output_aliases={} if out is None else {len(operands) - 1: 0},
        compiler_params=pltpu.CompilerParams(vmem_limit_bytes=vmem_limit),
        cost_estimate=pl.CostEstimate(flops=2 * share * plan.rank, bytes_accessed=4 * share, transcendentals=0),
        name="merge",
    )(*operands)


def on_device(shards, groups, base, narrow, wide, adapted_expert_index):
    rank = narrow.shape[3]
    rows, columns = narrow.shape[2], wide.shape[3]
    both, w = select(jnp.swapaxes(narrow, 2, 3), wide, adapted_expert_index)
    axes = ("shard", "group")

    if shards != 4 or groups != 4:
        n = lax.all_gather(both[:, :rows], "group", axis=1, tiled=True)
        w = lax.all_gather(w, axes, axis=1, tiled=True)
        whole = lambda s, g: 0
        plan = Plan(
            rank,
            columns * shards * groups,
            1,
            lambda s: 0,
            [(0, 0, rows * groups, whole)],
            [(1, 0, columns * shards * groups, whole)],
        )
        return merge(plan, base, [n, w])[0]

    def swap(x, axis, bit):
        return lax.ppermute(x, axis, [(i, i ^ bit) for i in range(4)])

    w3, w2, w1 = [swap(w, "shard", k) for k in (3, 2, 1)]
    base = load(base, w1)
    line = pack([w2, w3], (base,))
    own_a = pack([both, swap(both, "group", 2), w1, swap(w1, "group", 2)], (line,))
    other_a = swap(own_a, "group", 1)
    line_x = swap(line, "group", 2)
    half = rows + columns
    n_pieces = [
        (i, first, rows, lambda s, g, m=m: g ^ m)
        for i, first, m in ((0, 0, 0), (0, half, 2), (1, 0, 1), (1, half, 3))
    ]

    def w_piece(i, first, k, m):
        return (i, first, columns, lambda s, g: ((s ^ k) % 2) * groups + (g ^ m))

    near, far = [], []
    for i, m in ((0, 0), (1, 1)):
        near += [w_piece(i, rows, 0, m), w_piece(i, half + rows, 0, m ^ 2)]
        near += [w_piece(i, 2 * half, 1, m), w_piece(i, 2 * half + columns, 1, m ^ 2)]
        for at, k in ((0, 2), (1, 3)):
            far += [w_piece(i + 2, at * columns, k, m), w_piece(i + 2, (at + 2) * columns, k, m ^ 2)]
    span = 2 * columns * groups
    near_plan = Plan(rank, span, 2, lambda s: s // 2, n_pieces, near)
    far_plan = Plan(rank, span, 2, lambda s: 1 - s // 2, n_pieces, far)
    parts = [own_a, other_a]
    out, token = merge(near_plan, base, parts, after=(line,))
    own_b = pack([line, line_x], (token,))
    return merge(far_plan, base, parts + [own_b, swap(own_b, "group", 1)], out)[0]


def solution(mesh):
    return jax.shard_map(
        functools.partial(on_device, mesh.shape["shard"], mesh.shape["group"]),
        mesh=mesh,
        in_specs=(
            P("parts", None, "shard", None),
            P("parts", None, ("shard", "group"), None),
            P("parts", None, None, ("shard", "group")),
            P("parts"),
        ),
        out_specs=P("parts", None, "shard", None),
        check_vma=False,
    )
```

```python
import functools
import typing

import jax
import jax.numpy as jnp
from jax import lax
from jax.experimental import pallas as pl
from jax.experimental.pallas import tpu as pltpu
from jax.sharding import PartitionSpec as P

adapter_scale = 0.5
out_slots = 3
tile_rows = 512
in_vmem = pl.BlockSpec(memory_space=pltpu.VMEM)
in_hbm = pl.BlockSpec(memory_space=pltpu.HBM)
anywhere = pl.BlockSpec(memory_space=pl.ANY)
vmem_limit = 24 * 2**20


def select_kernel(index_ref, narrow_ref, wide_ref, both_out, w_out, index, n_buf, w_buf, index_sem, sems):
    experts = index_ref.shape[0]
    rank = narrow_ref.shape[2]
    rows = n_buf.shape[2]
    index_copy = pltpu.make_async_copy(index_ref, index, index_sem)
    index_copy.start()
    index_copy.wait()
    n_copies, w_copies = [], []
    for e in range(experts):
        i = index[e]
        ranks = pl.ds(e * rank, rank)
        w_copies.append(pltpu.make_async_copy(wide_ref.at[i], w_buf.at[:, ranks], sems.at[e, 1]))
        n_copies.append(pltpu.make_async_copy(narrow_ref.at[i], n_buf.at[:, ranks], sems.at[e, 0]))
    for copy in w_copies + n_copies:
        copy.start()
    for copy in w_copies:
        copy.wait()
    for p in range(w_buf.shape[0]):
        w = w_buf[p].astype(jnp.float32).T.astype(w_out.dtype)
        w_out[p] = w
        both_out[p, rows:] = w
    for copy in n_copies:
        copy.wait()
    for p in range(n_buf.shape[0]):
        n = n_buf[p].astype(jnp.float32) * adapter_scale
        both_out[p, :rows] = n.T.astype(both_out.dtype)


def select(narrow, wide, index):
    experts = index.shape[0]
    _, projections, rank, rows = narrow.shape
    columns = wide.shape[3]
    deep = experts * rank
    return pl.pallas_call(
        select_kernel,
        out_shape=(
            jax.ShapeDtypeStruct((projections, rows + columns, deep), narrow.dtype),
            jax.ShapeDtypeStruct((projections, columns, deep), wide.dtype),
        ),
        in_specs=[in_hbm] * 3,
        out_specs=[in_vmem] * 2,
        scratch_shapes=[
            pltpu.SMEM((experts,), index.dtype),
            pltpu.VMEM((projections, deep, rows), narrow.dtype),
            pltpu.VMEM((projections, deep, columns), wide.dtype),
            pltpu.SemaphoreType.DMA,
            pltpu.SemaphoreType.DMA((experts, 2)),
        ],
        compiler_params=pltpu.CompilerParams(vmem_limit_bytes=vmem_limit),
        name="select",
    )(*[pltpu.with_memory_space_constraint(x, pltpu.HBM) for x in (index, narrow, wide)])


def load_kernel(p, base_ref, *refs):
    out_ref, sem = refs[-2:]
    copy = pltpu.make_async_copy(base_ref.at[:, p], out_ref.at[:, p], sem)
    copy.start()
    copy.wait()


def load(base, p, loaded=None, after=()):
    extra = [*after] + ([] if loaded is None else [loaded])
    specs = [anywhere] * len(after) + ([] if loaded is None else [in_vmem])
    return pl.pallas_call(
        functools.partial(load_kernel, p),
        out_shape=jax.ShapeDtypeStruct(base.shape, base.dtype),
        in_specs=[in_hbm] + specs,
        out_specs=in_vmem,
        scratch_shapes=[pltpu.SemaphoreType.DMA],
        input_output_aliases={} if loaded is None else {len(extra): 0},
        compiler_params=pltpu.CompilerParams(vmem_limit_bytes=vmem_limit),
        cost_estimate=pl.CostEstimate(flops=0, bytes_accessed=2 * base.size // base.shape[1], transcendentals=0),
        name="load",
    )(pltpu.with_memory_space_constraint(base, pltpu.HBM), *extra)


def pack_kernel(count, *refs):
    out_ref = refs[-1]
    at = 0
    for ref in refs[:count]:
        rows = ref.shape[1]
        out_ref[:, at : at + rows] = ref[...]
        at += rows


def pack(blocks, after=()):
    projections, _, deep = blocks[0].shape
    rows = sum(x.shape[1] for x in blocks)
    return pl.pallas_call(
        functools.partial(pack_kernel, len(blocks)),
        out_shape=jax.ShapeDtypeStruct((projections, rows, deep), blocks[0].dtype),
        in_specs=[in_vmem] * len(blocks) + [anywhere] * len(after),
        out_specs=in_vmem,
        compiler_params=pltpu.CompilerParams(vmem_limit_bytes=vmem_limit),
        name="pack",
    )(*blocks, *after)


def merge_kernel(plan, late, *refs):
    base_ref, held_ref, *refs = refs if late else (None, *refs)
    n_all, w_all, out_buf, sems, late_sem = refs[-5:]
    out_ref, token, held_ref = refs[-8:-5] if late else [*refs[-7:-5], held_ref]
    experts, projections, width, _ = held_ref.shape
    _, span, deep = w_all.shape
    m_step = tile_rows if width % tile_rows == 0 else width
    f_step = 256 if span % 256 == 0 else span
    steps = projections * experts
    s, g = lax.axis_index("shard"), lax.axis_index("group")
    lane_expert = lax.broadcasted_iota(jnp.int32, (m_step, deep), 1) // plan.rank
    first_late = projections - late
    late_copies = [
        pltpu.make_async_copy(base_ref.at[:, p], held_ref.at[:, p], late_sem.at[p - first_late])
        for p in range(first_late, projections)
    ]
    for copy in late_copies:
        copy.start()

    def prepare(p, _):
        for i, first, rows, place in plan.n_pieces:
            at = pl.multiple_of(place(s, g) * rows, rows)
            n_all[p, pl.ds(at, rows), :] = refs[i][p, pl.ds(first, rows)]
        for i, first, rows, place in plan.w_pieces:
            at = pl.multiple_of(place(s, g) * rows, rows)
            w_all[p, pl.ds(at, rows), :] = refs[i][p, pl.ds(first, rows)]
        return 0

    lax.fori_loop(0, projections, prepare, 0)

    def merge_chunk(first_column):
        columns = pl.ds(first_column, span)

        def out_copies(step):
            p, e = step // experts, lax.rem(step, experts)
            slot = lax.rem(step, out_slots)
            return [
                pltpu.make_async_copy(
                    out_buf.at[slot, pl.ds(m, m_step)],
                    out_ref.at[e, p, pl.ds(m, m_step), columns],
                    sems.at[slot, m // m_step],
                )
                for m in range(0, width, m_step)
            ]

        def tile(step, _):
            p, e = step // experts, lax.rem(step, experts)
            slot = lax.rem(step, out_slots)

            @pl.when(step >= out_slots)
            def _():
                for copy in out_copies(step - out_slots):
                    copy.wait()

            for copy, m in zip(out_copies(step), range(0, width, m_step)):
                n = n_all[p, m : m + m_step, :]
                n = jnp.where(lane_expert == e, n, jnp.zeros_like(n))
                for f in range(0, span, f_step):
                    delta = lax.dot_general(
                        n, w_all[p, f : f + f_step], (((1,), (1,)), ((), ())), preferred_element_type=jnp.float32
                    )
                    b = held_ref[e, p, m : m + m_step, first_column + f : first_column + f + f_step]
                    out_buf[slot, m : m + m_step, f : f + f_step] = (b.astype(jnp.float32) + delta).astype(out_buf.dtype)
                copy.start()
            return 0

        lax.fori_loop(0, first_late * experts, tile, 0)
        if late:
            for copy in late_copies:
                copy.wait()
            lax.fori_loop(first_late * experts, steps, tile, 0)
        for step in range(max(0, steps - out_slots), steps):
            for copy in out_copies(jnp.int32(step)):
                copy.wait()

    for c in range(plan.chunks):
        pl.when(plan.chunk(s) == c)(functools.partial(merge_chunk, c * span))
    token[...] = jnp.zeros_like(token)


class Plan(typing.NamedTuple):
    rank: int
    span: int
    chunks: int
    chunk: typing.Callable
    n_pieces: list
    w_pieces: list


def merge(plan, base, held, parts, late=0, out=None, after=()):
    experts, projections, width, _ = held.shape
    deep = parts[0].shape[-1]
    share = projections * plan.span * experts * width
    extra = [*after] + ([] if out is None else [out])
    source = [pltpu.with_memory_space_constraint(base, pltpu.HBM)] if late else []
    operands = [*source, held, *parts, *extra]
    aliases = {} if out is None else {len(operands) - 1: 0}
    out_shape = [jax.ShapeDtypeStruct(held.shape, held.dtype), jax.ShapeDtypeStruct((8, 128), jnp.float32)]
    out_specs = [in_hbm, in_vmem]
    if late:
        aliases[1] = 2
        out_shape.append(jax.ShapeDtypeStruct(held.shape, held.dtype))
        out_specs.append(in_vmem)
    return pl.pallas_call(
        functools.partial(merge_kernel, plan, late),
        out_shape=out_shape,
        in_specs=[in_hbm] * len(source) + [in_vmem] * (1 + len(parts)) + [anywhere] * len(extra),
        out_specs=out_specs,
        scratch_shapes=[
            pltpu.VMEM((projections, width, deep), held.dtype),
            pltpu.VMEM((projections, plan.span, deep), held.dtype),
            pltpu.VMEM((out_slots, width, plan.span), held.dtype),
            pltpu.SemaphoreType.DMA((out_slots, 2)),
            pltpu.SemaphoreType.DMA((max(late, 1),)),
        ],
        input_output_aliases=aliases,
        compiler_params=pltpu.CompilerParams(vmem_limit_bytes=vmem_limit),
        cost_estimate=pl.CostEstimate(flops=2 * share * plan.rank, bytes_accessed=4 * share, transcendentals=0),
        name="merge",
    )(*operands)


def on_device(shards, groups, base, narrow, wide, adapted_expert_index):
    rank = narrow.shape[3]
    rows, columns = narrow.shape[2], wide.shape[3]
    both, w = select(jnp.swapaxes(narrow, 2, 3), wide, adapted_expert_index)
    axes = ("shard", "group")

    if shards != 4 or groups != 4:
        n = lax.all_gather(both[:, :rows], "group", axis=1, tiled=True)
        w = lax.all_gather(w, axes, axis=1, tiled=True)
        whole = lambda s, g: 0
        plan = Plan(
            rank,
            columns * shards * groups,
            1,
            lambda s: 0,
            [(0, 0, rows * groups, whole)],
            [(1, 0, columns * shards * groups, whole)],
        )
        return merge(plan, None, base, [n, w])[0]

    def swap(x, axis, bit):
        return lax.ppermute(x, axis, [(i, i ^ bit) for i in range(4)])

    w2, w1 = [swap(w, "shard", k) for k in (2, 1)]
    held = load(base, 0, after=(w1,))
    w2 = pack([w2], (held,))
    held = load(base, 1, held, (w2,))
    line = pack([w2, swap(w2, "shard", 1)], (held,))
    own_a = pack([both, swap(both, "group", 2), w1, swap(w1, "group", 2)], (line,))
    other_a = swap(own_a, "group", 1)
    line_x = swap(line, "group", 2)
    half = rows + columns
    n_pieces = [
        (i, first, rows, lambda s, g, m=m: g ^ m)
        for i, first, m in ((0, 0, 0), (0, half, 2), (1, 0, 1), (1, half, 3))
    ]

    def w_piece(i, first, k, m):
        return (i, first, columns, lambda s, g: ((s ^ k) % 2) * groups + (g ^ m))

    near, far = [], []
    for i, m in ((0, 0), (1, 1)):
        near += [w_piece(i, rows, 0, m), w_piece(i, half + rows, 0, m ^ 2)]
        near += [w_piece(i, 2 * half, 1, m), w_piece(i, 2 * half + columns, 1, m ^ 2)]
        for at, k in ((0, 2), (1, 3)):
            far += [w_piece(i + 2, at * columns, k, m), w_piece(i + 2, (at + 2) * columns, k, m ^ 2)]
    span = 2 * columns * groups
    near_plan = Plan(rank, span, 2, lambda s: s // 2, n_pieces, near)
    far_plan = Plan(rank, span, 2, lambda s: 1 - s // 2, n_pieces, far)
    parts = [own_a, other_a]
    out, token, held = merge(near_plan, base, held, parts, 1, after=(line,))
    own_b = pack([line, line_x], (token,))
    return merge(far_plan, None, held, parts + [own_b, swap(own_b, "group", 1)], out=out)[0]


def solution(mesh):
    return jax.shard_map(
        functools.partial(on_device, mesh.shape["shard"], mesh.shape["group"]),
        mesh=mesh,
        in_specs=(
            P("parts", None, "shard", None),
            P("parts", None, ("shard", "group"), None),
            P("parts", None, None, ("shard", "group")),
            P("parts"),
        ),
        out_specs=P("parts", None, "shard", None),
        check_vma=False,
    )
```

```python
import functools
import typing

import jax
import jax.numpy as jnp
from jax import lax
from jax.experimental import pallas as pl
from jax.experimental.pallas import tpu as pltpu
from jax.sharding import PartitionSpec as P

adapter_scale = 0.5
out_slots = 3
tile_rows = 512
in_vmem = pl.BlockSpec(memory_space=pltpu.VMEM)
in_hbm = pl.BlockSpec(memory_space=pltpu.HBM)
anywhere = pl.BlockSpec(memory_space=pl.ANY)
vmem_limit = 24 * 2**20


def held_copy(base_ref, held_ref, first, last, sem):
    rows = pl.ds(first, last - first)
    return pltpu.make_async_copy(base_ref.at[:, :, rows], held_ref.at[:, :, rows], sem)


def select_kernel(early, index_ref, narrow_ref, wide_ref, *refs):
    both_out, w_out = refs[:2]
    index, n_buf, w_buf, index_sem, sems, early_sem = refs[-6:]
    experts = index_ref.shape[0]
    rank = narrow_ref.shape[2]
    rows = n_buf.shape[2]
    index_copy = pltpu.make_async_copy(index_ref, index, index_sem)
    index_copy.start()
    index_copy.wait()
    n_copies, w_copies = [], []
    for e in range(experts):
        i = index[e]
        ranks = pl.ds(e * rank, rank)
        w_copies.append(pltpu.make_async_copy(wide_ref.at[i], w_buf.at[:, ranks], sems.at[e, 1]))
        n_copies.append(pltpu.make_async_copy(narrow_ref.at[i], n_buf.at[:, ranks], sems.at[e, 0]))
    for copy in w_copies + n_copies:
        copy.start()
    if early:
        base_ref, held_ref = refs[2:4]
        early_copy = held_copy(base_ref, held_ref, 0, early, early_sem)
        early_copy.start()
    for copy in w_copies:
        copy.wait()
    for p in range(w_buf.shape[0]):
        w = w_buf[p].astype(jnp.float32).T.astype(w_out.dtype)
        w_out[p] = w
        both_out[p, rows:] = w
    for copy in n_copies:
        copy.wait()
    for p in range(n_buf.shape[0]):
        n = n_buf[p].astype(jnp.float32) * adapter_scale
        both_out[p, :rows] = n.T.astype(both_out.dtype)
    if early:
        early_copy.wait()


def select(narrow, wide, index, base=None, early=0):
    experts = index.shape[0]
    _, projections, rank, rows = narrow.shape
    columns = wide.shape[3]
    deep = experts * rank
    operands = [index, narrow, wide] + ([base] if early else [])
    out_shape = [
        jax.ShapeDtypeStruct((projections, rows + columns, deep), narrow.dtype),
        jax.ShapeDtypeStruct((projections, columns, deep), wide.dtype),
    ] + ([jax.ShapeDtypeStruct(base.shape, base.dtype)] if early else [])

    def kernel(*refs):
        inputs, outputs, scratch = refs[:3], refs[len(operands) : -6], refs[-6:]
        select_kernel(early, *inputs, *outputs[:2], *refs[3 : len(operands)], *outputs[2:], *scratch)

    return pl.pallas_call(
        kernel,
        out_shape=out_shape,
        in_specs=[in_hbm] * len(operands),
        out_specs=[in_vmem] * len(out_shape),
        scratch_shapes=[
            pltpu.SMEM((experts,), index.dtype),
            pltpu.VMEM((projections, deep, rows), narrow.dtype),
            pltpu.VMEM((projections, deep, columns), wide.dtype),
            pltpu.SemaphoreType.DMA,
            pltpu.SemaphoreType.DMA((experts, 2)),
            pltpu.SemaphoreType.DMA,
        ],
        compiler_params=pltpu.CompilerParams(vmem_limit_bytes=vmem_limit),
        name="select",
    )(*[pltpu.with_memory_space_constraint(x, pltpu.HBM) for x in operands])


def load_kernel(early, base_ref, _, __, out_ref, sem):
    copy = held_copy(base_ref, out_ref, early, out_ref.shape[2], sem)
    copy.start()
    copy.wait()


def load(base, held, early, after):
    return pl.pallas_call(
        functools.partial(load_kernel, early),
        out_shape=jax.ShapeDtypeStruct(base.shape, base.dtype),
        in_specs=[in_hbm, in_vmem, anywhere],
        out_specs=in_vmem,
        scratch_shapes=[pltpu.SemaphoreType.DMA],
        input_output_aliases={1: 0},
        compiler_params=pltpu.CompilerParams(vmem_limit_bytes=vmem_limit),
        cost_estimate=pl.CostEstimate(flops=0, bytes_accessed=2 * base.size, transcendentals=0),
        name="load",
    )(pltpu.with_memory_space_constraint(base, pltpu.HBM), held, after)


def pack_kernel(count, *refs):
    out_ref = refs[-1]
    at = 0
    for ref in refs[:count]:
        rows = ref.shape[1]
        out_ref[:, at : at + rows] = ref[...]
        at += rows


def pack(blocks, after=()):
    projections, _, deep = blocks[0].shape
    rows = sum(x.shape[1] for x in blocks)
    return pl.pallas_call(
        functools.partial(pack_kernel, len(blocks)),
        out_shape=jax.ShapeDtypeStruct((projections, rows, deep), blocks[0].dtype),
        in_specs=[in_vmem] * len(blocks) + [anywhere] * len(after),
        out_specs=in_vmem,
        compiler_params=pltpu.CompilerParams(vmem_limit_bytes=vmem_limit),
        name="pack",
    )(*blocks, *after)


def merge_kernel(plan, held_ref, *refs):
    out_ref, token, n_all, w_all, out_buf, sems = refs[-6:]
    experts, projections, width, _ = held_ref.shape
    _, span, deep = w_all.shape
    m_step = tile_rows if width % tile_rows == 0 else width
    f_step = 256 if span % 256 == 0 else span
    steps = projections * experts
    s, g = lax.axis_index("shard"), lax.axis_index("group")
    lane_expert = lax.broadcasted_iota(jnp.int32, (m_step, deep), 1) // plan.rank

    def prepare(p, _):
        for i, first, rows, place in plan.n_pieces:
            at = pl.multiple_of(place(s, g) * rows, rows)
            n_all[p, pl.ds(at, rows), :] = refs[i][p, pl.ds(first, rows)]
        for i, first, rows, place in plan.w_pieces:
            at = pl.multiple_of(place(s, g) * rows, rows)
            w_all[p, pl.ds(at, rows), :] = refs[i][p, pl.ds(first, rows)]
        return 0

    lax.fori_loop(0, projections, prepare, 0)

    def merge_chunk(first_column):
        columns = pl.ds(first_column, span)

        def out_copies(step):
            p, e = step // experts, lax.rem(step, experts)
            slot = lax.rem(step, out_slots)
            return [
                pltpu.make_async_copy(
                    out_buf.at[slot, pl.ds(m, m_step)],
                    out_ref.at[e, p, pl.ds(m, m_step), columns],
                    sems.at[slot, m // m_step],
                )
                for m in range(0, width, m_step)
            ]

        def tile(step, _):
            p, e = step // experts, lax.rem(step, experts)
            slot = lax.rem(step, out_slots)

            @pl.when(step >= out_slots)
            def _():
                for copy in out_copies(step - out_slots):
                    copy.wait()

            for copy, m in zip(out_copies(step), range(0, width, m_step)):
                n = n_all[p, m : m + m_step, :]
                n = jnp.where(lane_expert == e, n, jnp.zeros_like(n))
                for f in range(0, span, f_step):
                    delta = lax.dot_general(
                        n, w_all[p, f : f + f_step], (((1,), (1,)), ((), ())), preferred_element_type=jnp.float32
                    )
                    b = held_ref[e, p, m : m + m_step, first_column + f : first_column + f + f_step]
                    out_buf[slot, m : m + m_step, f : f + f_step] = (b.astype(jnp.float32) + delta).astype(out_buf.dtype)
                copy.start()
            return 0

        lax.fori_loop(0, steps, tile, 0)
        for step in range(max(0, steps - out_slots), steps):
            for copy in out_copies(jnp.int32(step)):
                copy.wait()

    for c in range(plan.chunks):
        pl.when(plan.chunk(s) == c)(functools.partial(merge_chunk, c * span))
    token[...] = jnp.zeros_like(token)


class Plan(typing.NamedTuple):
    rank: int
    span: int
    chunks: int
    chunk: typing.Callable
    n_pieces: list
    w_pieces: list


def merge(plan, held, parts, out=None, after=()):
    experts, projections, width, _ = held.shape
    deep = parts[0].shape[-1]
    share = projections * plan.span * experts * width
    extra = [*after] + ([] if out is None else [out])
    operands = [held, *parts, *extra]
    return pl.pallas_call(
        functools.partial(merge_kernel, plan),
        out_shape=[jax.ShapeDtypeStruct(held.shape, held.dtype), jax.ShapeDtypeStruct((8, 128), jnp.float32)],
        in_specs=[in_vmem] * (1 + len(parts)) + [anywhere] * len(extra),
        out_specs=[in_hbm, in_vmem],
        scratch_shapes=[
            pltpu.VMEM((projections, width, deep), held.dtype),
            pltpu.VMEM((projections, plan.span, deep), held.dtype),
            pltpu.VMEM((out_slots, width, plan.span), held.dtype),
            pltpu.SemaphoreType.DMA((out_slots, 2)),
        ],
        input_output_aliases={} if out is None else {len(operands) - 1: 0},
        compiler_params=pltpu.CompilerParams(vmem_limit_bytes=vmem_limit),
        cost_estimate=pl.CostEstimate(flops=2 * share * plan.rank, bytes_accessed=4 * share, transcendentals=0),
        name="merge",
    )(*operands)


def on_device(shards, groups, base, narrow, wide, adapted_expert_index):
    rank = narrow.shape[3]
    rows, columns = narrow.shape[2], wide.shape[3]
    axes = ("shard", "group")
    narrow = jnp.swapaxes(narrow, 2, 3)

    if shards != 4 or groups != 4:
        both, w = select(narrow, wide, adapted_expert_index)
        n = lax.all_gather(both[:, :rows], "group", axis=1, tiled=True)
        w = lax.all_gather(w, axes, axis=1, tiled=True)
        whole = lambda s, g: 0
        n_pieces = [(0, 0, rows * groups, whole)]
        w_pieces = [(1, 0, columns * shards * groups, whole)]
        plan = Plan(rank, columns * shards * groups, 1, lambda s: 0, n_pieces, w_pieces)
        return merge(plan, base, [n, w])[0]

    def swap(x, axis, bit):
        return lax.ppermute(x, axis, [(i, i ^ bit) for i in range(4)])

    early = rows
    both, w, held = select(narrow, wide, adapted_expert_index, base, early)
    w3, w2, w1 = [swap(w, "shard", k) for k in (3, 2, 1)]
    held = load(base, held, early, w1)
    line = pack([w2, w3], (held,))
    own_a = pack([both, swap(both, "group", 2), w1, swap(w1, "group", 2)], (line,))
    other_a = swap(own_a, "group", 1)
    line_x = swap(line, "group", 2)
    half = rows + columns
    n_pieces = [
        (i, first, rows, lambda s, g, m=m: g ^ m)
        for i, first, m in ((0, 0, 0), (0, half, 2), (1, 0, 1), (1, half, 3))
    ]

    def w_piece(i, first, k, m):
        return (i, first, columns, lambda s, g: ((s ^ k) % 2) * groups + (g ^ m))

    near, far = [], []
    for i, m in ((0, 0), (1, 1)):
        near += [w_piece(i, rows, 0, m), w_piece(i, half + rows, 0, m ^ 2)]
        near += [w_piece(i, 2 * half, 1, m), w_piece(i, 2 * half + columns, 1, m ^ 2)]
        for at, k in ((0, 2), (1, 3)):
            far += [w_piece(i + 2, at * columns, k, m), w_piece(i + 2, (at + 2) * columns, k, m ^ 2)]
    span = 2 * columns * groups
    near_plan = Plan(rank, span, 2, lambda s: s // 2, n_pieces, near)
    far_plan = Plan(rank, span, 2, lambda s: 1 - s // 2, n_pieces, far)
    parts = [own_a, other_a]
    out, token = merge(near_plan, held, parts, after=(line,))
    own_b = pack([line, line_x], (token,))
    return merge(far_plan, held, parts + [own_b, swap(own_b, "group", 1)], out)[0]


def solution(mesh):
    return jax.shard_map(
        functools.partial(on_device, mesh.shape["shard"], mesh.shape["group"]),
        mesh=mesh,
        in_specs=(
            P("parts", None, "shard", None),
            P("parts", None, ("shard", "group"), None),
            P("parts", None, None, ("shard", "group")),
            P("parts"),
        ),
        out_specs=P("parts", None, "shard", None),
        check_vma=False,
    )
```

```python
import functools
import typing

import jax
import jax.numpy as jnp
from jax import lax
from jax.experimental import pallas as pl
from jax.experimental.pallas import tpu as pltpu
from jax.sharding import PartitionSpec as P

adapter_scale = 0.5
out_slots = 4
tile_rows = 512
in_vmem = pl.BlockSpec(memory_space=pltpu.VMEM)
in_hbm = pl.BlockSpec(memory_space=pltpu.HBM)
anywhere = pl.BlockSpec(memory_space=pl.ANY)
vmem_limit = 24 * 2**20


def select_kernel(index_ref, narrow_ref, wide_ref, both_out, w_out, index, n_buf, w_buf, index_sem, sems):
    experts = index_ref.shape[0]
    rank = narrow_ref.shape[2]
    rows = n_buf.shape[2]
    index_copy = pltpu.make_async_copy(index_ref, index, index_sem)
    index_copy.start()
    index_copy.wait()
    n_copies, w_copies = [], []
    for e in range(experts):
        i = index[e]
        ranks = pl.ds(e * rank, rank)
        w_copies.append(pltpu.make_async_copy(wide_ref.at[i], w_buf.at[:, ranks], sems.at[e, 1]))
        n_copies.append(pltpu.make_async_copy(narrow_ref.at[i], n_buf.at[:, ranks], sems.at[e, 0]))
    for copy in w_copies + n_copies:
        copy.start()
    for copy in w_copies:
        copy.wait()
    for p in range(w_buf.shape[0]):
        w = w_buf[p].astype(jnp.float32).T.astype(w_out.dtype)
        w_out[p] = w
        both_out[p, rows:] = w
    for copy in n_copies:
        copy.wait()
    for p in range(n_buf.shape[0]):
        n = n_buf[p].astype(jnp.float32) * adapter_scale
        both_out[p, :rows] = n.T.astype(both_out.dtype)


def select(narrow, wide, index):
    experts = index.shape[0]
    _, projections, rank, rows = narrow.shape
    columns = wide.shape[3]
    deep = experts * rank
    return pl.pallas_call(
        select_kernel,
        out_shape=(
            jax.ShapeDtypeStruct((projections, rows + columns, deep), narrow.dtype),
            jax.ShapeDtypeStruct((projections, columns, deep), wide.dtype),
        ),
        in_specs=[in_hbm] * 3,
        out_specs=[in_vmem] * 2,
        scratch_shapes=[
            pltpu.SMEM((experts,), index.dtype),
            pltpu.VMEM((projections, deep, rows), narrow.dtype),
            pltpu.VMEM((projections, deep, columns), wide.dtype),
            pltpu.SemaphoreType.DMA,
            pltpu.SemaphoreType.DMA((experts, 2)),
        ],
        compiler_params=pltpu.CompilerParams(vmem_limit_bytes=vmem_limit),
        name="select",
    )(*[pltpu.with_memory_space_constraint(x, pltpu.HBM) for x in (index, narrow, wide)])


def load_kernel(first, last, base_ref, *refs):
    out_ref, sem = refs[-2:]
    rows = pl.ds(first, last - first)
    copy = pltpu.make_async_copy(base_ref.at[:, :, rows], out_ref.at[:, :, rows], sem)
    copy.start()
    copy.wait()


def load(base, first, last, after, held=None):
    operands = [pltpu.with_memory_space_constraint(base, pltpu.HBM), after] + ([] if held is None else [held])
    return pl.pallas_call(
        functools.partial(load_kernel, first, last),
        out_shape=jax.ShapeDtypeStruct(base.shape, base.dtype),
        in_specs=[in_hbm, anywhere, in_vmem][: len(operands)],
        out_specs=in_vmem,
        scratch_shapes=[pltpu.SemaphoreType.DMA],
        input_output_aliases={} if held is None else {2: 0},
        compiler_params=pltpu.CompilerParams(vmem_limit_bytes=vmem_limit),
        cost_estimate=pl.CostEstimate(flops=0, bytes_accessed=2 * base.size, transcendentals=0),
        name="load",
    )(*operands)


def pack_kernel(count, *refs):
    out_ref = refs[-1]
    at = 0
    for ref in refs[:count]:
        rows = ref.shape[1]
        out_ref[:, at : at + rows] = ref[...]
        at += rows


def pack(blocks, after=()):
    projections, _, deep = blocks[0].shape
    rows = sum(x.shape[1] for x in blocks)
    return pl.pallas_call(
        functools.partial(pack_kernel, len(blocks)),
        out_shape=jax.ShapeDtypeStruct((projections, rows, deep), blocks[0].dtype),
        in_specs=[in_vmem] * len(blocks) + [anywhere] * len(after),
        out_specs=in_vmem,
        compiler_params=pltpu.CompilerParams(vmem_limit_bytes=vmem_limit),
        name="pack",
    )(*blocks, *after)


def merge_kernel(plan, held_ref, *refs):
    out_ref, n_all, w_all, out_buf, sems = refs[-5:]
    experts, projections, width, wide_columns = held_ref.shape
    deep = n_all.shape[2]
    m_step = out_buf.shape[1]
    f_step = 256 if wide_columns % 256 == 0 else wide_columns
    strips = width // m_step
    tiles = experts * strips
    steps = projections * tiles
    s, g = lax.axis_index("shard"), lax.axis_index("group")
    lane_expert = lax.broadcasted_iota(jnp.int32, (m_step, deep), 1) // plan.rank

    def prepare(p, _):
        for pieces, whole in ((plan.n_pieces, n_all), (plan.w_pieces, w_all)):
            for i, first, rows, place in pieces:
                at = pl.multiple_of(place(s, g) * rows, rows)
                whole[p, pl.ds(at, rows), :] = refs[i][p, pl.ds(first, rows)]
        return 0

    def where(step):
        p, t = step // tiles, lax.rem(step, tiles)
        rows = pl.ds(pl.multiple_of(lax.rem(t, strips) * m_step, m_step), m_step)
        return t // strips, p, rows, lax.rem(step, out_slots)

    def out_copy(step):
        e, p, rows, slot = where(step)
        return pltpu.make_async_copy(out_buf.at[slot], out_ref.at[e, p, rows], sems.at[slot])

    def tile(step, _):
        e, p, rows, slot = where(step)

        @pl.when(step >= out_slots)
        def _():
            out_copy(step - out_slots).wait()

        n = n_all[p, rows, :]
        n = jnp.where(lane_expert == e, n, jnp.zeros_like(n))
        for f in range(0, wide_columns, f_step):
            delta = lax.dot_general(
                n, w_all[p, f : f + f_step], (((1,), (1,)), ((), ())), preferred_element_type=jnp.float32
            )
            b = held_ref[e, p, rows, f : f + f_step].astype(jnp.float32)
            out_buf[slot, :, f : f + f_step] = (b + delta).astype(out_buf.dtype)
        out_copy(step).start()
        return 0

    lax.fori_loop(0, projections, prepare, 0)
    lax.fori_loop(0, steps, tile, 0)
    for step in range(max(0, steps - out_slots), steps):
        out_copy(jnp.int32(step)).wait()


class Plan(typing.NamedTuple):
    rank: int
    n_pieces: list
    w_pieces: list


def merge(plan, held, parts):
    experts, projections, width, wide_columns = held.shape
    deep = parts[0].shape[-1]
    m_step = tile_rows if width % tile_rows == 0 else width
    return pl.pallas_call(
        functools.partial(merge_kernel, plan),
        out_shape=jax.ShapeDtypeStruct(held.shape, held.dtype),
        in_specs=[in_vmem] * (1 + len(parts)),
        out_specs=in_hbm,
        scratch_shapes=[
            pltpu.VMEM((projections, width, deep), held.dtype),
            pltpu.VMEM((projections, wide_columns, deep), held.dtype),
            pltpu.VMEM((out_slots, m_step, wide_columns), held.dtype),
            pltpu.SemaphoreType.DMA((out_slots,)),
        ],
        compiler_params=pltpu.CompilerParams(vmem_limit_bytes=vmem_limit),
        cost_estimate=pl.CostEstimate(
            flops=2 * held.size * plan.rank, bytes_accessed=4 * held.size, transcendentals=0
        ),
        name="merge",
    )(held, *parts)


def on_device(shards, groups, base, narrow, wide, adapted_expert_index):
    rank = narrow.shape[3]
    rows, columns = narrow.shape[2], wide.shape[3]
    axes = ("shard", "group")
    narrow = jnp.swapaxes(narrow, 2, 3)

    if shards != 4 or groups != 4:
        both, w = select(narrow, wide, adapted_expert_index)
        n = lax.all_gather(both[:, :rows], "group", axis=1, tiled=True)
        w = lax.all_gather(w, axes, axis=1, tiled=True)
        whole = lambda s, g: 0
        n_pieces = [(0, 0, rows * groups, whole)]
        w_pieces = [(1, 0, columns * shards * groups, whole)]
        return merge(Plan(rank, n_pieces, w_pieces), base, [n, w])

    def swap(x, axis, bit):
        return lax.ppermute(x, axis, [(i, i ^ bit) for i in range(4)])

    both, w = select(narrow, wide, adapted_expert_index)
    w3, w2, w1 = [swap(w, "shard", k) for k in (3, 2, 1)]
    both_x = swap(pack([both], (w1,)), "group", 2)
    split = base.shape[2] * 3 // 8
    held = load(base, 0, split, w1)
    line = pack([w1, w2, w3], (held,))
    own = pack([both, line])
    held = load(base, split, base.shape[2], line, held)
    both_x = pack([both_x], (held,))
    parts = [own, both_x, swap(line, "group", 2)]
    parts += [swap(x, "group", 1) for x in parts]
    n_pieces, w_pieces = [], []
    for i, m in ((0, 0), (3, 1)):
        n_pieces += [(i, 0, rows, lambda s, g, m=m: g ^ m), (i + 1, 0, rows, lambda s, g, m=m: g ^ m ^ 2)]
        for k in range(4):
            place = lambda s, g, m=m, k=k: (s ^ k) * groups + (g ^ m)
            place_x = lambda s, g, m=m, k=k: (s ^ k) * groups + (g ^ m ^ 2)
            w_pieces.append((i, rows + k * columns, columns, place))
            w_pieces.append((i + 1, rows, columns, place_x) if k == 0 else (i + 2, (k - 1) * columns, columns, place_x))
    return merge(Plan(rank, n_pieces, w_pieces), held, parts)


def solution(mesh):
    return jax.shard_map(
        functools.partial(on_device, mesh.shape["shard"], mesh.shape["group"]),
        mesh=mesh,
        in_specs=(
            P("parts", None, "shard", None),
            P("parts", None, ("shard", "group"), None),
            P("parts", None, None, ("shard", "group")),
            P("parts"),
        ),
        out_specs=P("parts", None, "shard", None),
        check_vma=False,
    )
```

```python
import functools
import typing

import jax
import jax.numpy as jnp
from jax import lax
from jax.experimental import pallas as pl
from jax.experimental.pallas import tpu as pltpu
from jax.sharding import PartitionSpec as P

adapter_scale = 0.5
out_slots = 3
tile_rows = 512
in_vmem = pl.BlockSpec(memory_space=pltpu.VMEM)
in_hbm = pl.BlockSpec(memory_space=pltpu.HBM)
anywhere = pl.BlockSpec(memory_space=pl.ANY)
vmem_limit = 24 * 2**20


def select_kernel(index_ref, narrow_ref, wide_ref, both_out, w_out, index, n_buf, w_buf, index_sem, sems):
    experts = index_ref.shape[0]
    rank = narrow_ref.shape[2]
    rows = n_buf.shape[2]
    index_copy = pltpu.make_async_copy(index_ref, index, index_sem)
    index_copy.start()
    index_copy.wait()
    n_copies, w_copies = [], []
    for e in range(experts):
        i = index[e]
        ranks = pl.ds(e * rank, rank)
        w_copies.append(pltpu.make_async_copy(wide_ref.at[i], w_buf.at[:, ranks], sems.at[e, 1]))
        n_copies.append(pltpu.make_async_copy(narrow_ref.at[i], n_buf.at[:, ranks], sems.at[e, 0]))
    for copy in w_copies + n_copies:
        copy.start()
    for copy in w_copies:
        copy.wait()
    for p in range(w_buf.shape[0]):
        w = w_buf[p].astype(jnp.float32).T.astype(w_out.dtype)
        w_out[p] = w
        both_out[p, rows:] = w
    for copy in n_copies:
        copy.wait()
    for p in range(n_buf.shape[0]):
        n = n_buf[p].astype(jnp.float32) * adapter_scale
        both_out[p, :rows] = n.T.astype(both_out.dtype)


def select(narrow, wide, index):
    experts = index.shape[0]
    _, projections, rank, rows = narrow.shape
    columns = wide.shape[3]
    deep = experts * rank
    return pl.pallas_call(
        select_kernel,
        out_shape=(
            jax.ShapeDtypeStruct((projections, rows + columns, deep), narrow.dtype),
            jax.ShapeDtypeStruct((projections, columns, deep), wide.dtype),
        ),
        in_specs=[in_hbm] * 3,
        out_specs=[in_vmem] * 2,
        scratch_shapes=[
            pltpu.SMEM((experts,), index.dtype),
            pltpu.VMEM((projections, deep, rows), narrow.dtype),
            pltpu.VMEM((projections, deep, columns), wide.dtype),
            pltpu.SemaphoreType.DMA,
            pltpu.SemaphoreType.DMA((experts, 2)),
        ],
        compiler_params=pltpu.CompilerParams(vmem_limit_bytes=vmem_limit),
        name="select",
    )(*[pltpu.with_memory_space_constraint(x, pltpu.HBM) for x in (index, narrow, wide)])


def load_kernel(blocks, base_ref, *refs):
    out_ref, sems = refs[-2:]
    s = lax.axis_index("shard")
    copies = []
    for n, (chunk, span, first, last) in enumerate(blocks):
        columns = pl.ds(pl.multiple_of(chunk(s) * span, span), span)
        rows = pl.ds(first, last - first)
        copies.append(
            pltpu.make_async_copy(base_ref.at[:, :, rows, columns], out_ref.at[:, :, rows, columns], sems.at[n])
        )
    for copy in copies:
        copy.start()
    for copy in copies:
        copy.wait()


def load(base, blocks, after, held=None):
    operands = [pltpu.with_memory_space_constraint(base, pltpu.HBM), after] + ([] if held is None else [held])
    return pl.pallas_call(
        functools.partial(load_kernel, blocks),
        out_shape=jax.ShapeDtypeStruct(base.shape, base.dtype),
        in_specs=[in_hbm, anywhere, in_vmem][: len(operands)],
        out_specs=in_vmem,
        scratch_shapes=[pltpu.SemaphoreType.DMA((len(blocks),))],
        input_output_aliases={} if held is None else {2: 0},
        compiler_params=pltpu.CompilerParams(vmem_limit_bytes=vmem_limit),
        cost_estimate=pl.CostEstimate(flops=0, bytes_accessed=2 * base.size, transcendentals=0),
        name="load",
    )(*operands)


def pack_kernel(count, *refs):
    out_ref = refs[-1]
    at = 0
    for ref in refs[:count]:
        rows = ref.shape[1]
        out_ref[:, at : at + rows] = ref[...]
        at += rows


def pack(blocks, after=()):
    projections, _, deep = blocks[0].shape
    rows = sum(x.shape[1] for x in blocks)
    return pl.pallas_call(
        functools.partial(pack_kernel, len(blocks)),
        out_shape=jax.ShapeDtypeStruct((projections, rows, deep), blocks[0].dtype),
        in_specs=[in_vmem] * len(blocks) + [anywhere] * len(after),
        out_specs=in_vmem,
        compiler_params=pltpu.CompilerParams(vmem_limit_bytes=vmem_limit),
        name="pack",
    )(*blocks, *after)


def merge_kernel(plan, held_ref, *refs):
    out_ref, token, n_all, w_all, out_buf, sems = refs[-6:]
    experts, projections, width, _ = held_ref.shape
    _, span, deep = w_all.shape
    m_step = tile_rows if width % tile_rows == 0 else width
    f_step = 256 if span % 256 == 0 else span
    steps = projections * experts
    s, g = lax.axis_index("shard"), lax.axis_index("group")
    lane_expert = lax.broadcasted_iota(jnp.int32, (m_step, deep), 1) // plan.rank

    def prepare(p, _):
        for i, first, rows, place in plan.n_pieces:
            at = pl.multiple_of(place(s, g) * rows, rows)
            n_all[p, pl.ds(at, rows), :] = refs[i][p, pl.ds(first, rows)]
        for i, first, rows, place in plan.w_pieces:
            at = pl.multiple_of(place(s, g) * rows, rows)
            w_all[p, pl.ds(at, rows), :] = refs[i][p, pl.ds(first, rows)]
        return 0

    lax.fori_loop(0, projections, prepare, 0)

    def merge_chunk(first_column):
        columns = pl.ds(first_column, span)

        def out_copies(step):
            p, e = step // experts, lax.rem(step, experts)
            slot = lax.rem(step, out_slots)
            return [
                pltpu.make_async_copy(
                    out_buf.at[slot, pl.ds(m, m_step)],
                    out_ref.at[e, p, pl.ds(m, m_step), columns],
                    sems.at[slot, m // m_step],
                )
                for m in range(0, width, m_step)
            ]

        def tile(step, _):
            p, e = step // experts, lax.rem(step, experts)
            slot = lax.rem(step, out_slots)

            @pl.when(step >= out_slots)
            def _():
                for copy in out_copies(step - out_slots):
                    copy.wait()

            for copy, m in zip(out_copies(step), range(0, width, m_step)):
                n = n_all[p, m : m + m_step, :]
                n = jnp.where(lane_expert == e, n, jnp.zeros_like(n))
                for f in range(0, span, f_step):
                    delta = lax.dot_general(
                        n, w_all[p, f : f + f_step], (((1,), (1,)), ((), ())), preferred_element_type=jnp.float32
                    )
                    b = held_ref[e, p, m : m + m_step, first_column + f : first_column + f + f_step]
                    out_buf[slot, m : m + m_step, f : f + f_step] = (b.astype(jnp.float32) + delta).astype(out_buf.dtype)
                copy.start()
            return 0

        lax.fori_loop(0, steps, tile, 0)
        for step in range(max(0, steps - out_slots), steps):
            for copy in out_copies(jnp.int32(step)):
                copy.wait()

    for c in range(plan.chunks):
        pl.when(plan.chunk(s) == c)(functools.partial(merge_chunk, c * span))
    token[...] = jnp.zeros_like(token)


class Plan(typing.NamedTuple):
    rank: int
    span: int
    chunks: int
    chunk: typing.Callable
    n_pieces: list
    w_pieces: list


def merge(plan, held, parts, out=None, after=()):
    experts, projections, width, _ = held.shape
    deep = parts[0].shape[-1]
    share = projections * plan.span * experts * width
    extra = [*after] + ([] if out is None else [out])
    operands = [held, *parts, *extra]
    return pl.pallas_call(
        functools.partial(merge_kernel, plan),
        out_shape=[jax.ShapeDtypeStruct(held.shape, held.dtype), jax.ShapeDtypeStruct((8, 128), jnp.float32)],
        in_specs=[in_vmem] * (1 + len(parts)) + [anywhere] * len(extra),
        out_specs=[in_hbm, in_vmem],
        scratch_shapes=[
            pltpu.VMEM((projections, width, deep), held.dtype),
            pltpu.VMEM((projections, plan.span, deep), held.dtype),
            pltpu.VMEM((out_slots, width, plan.span), held.dtype),
            pltpu.SemaphoreType.DMA((out_slots, 2)),
        ],
        input_output_aliases={} if out is None else {len(operands) - 1: 0},
        compiler_params=pltpu.CompilerParams(vmem_limit_bytes=vmem_limit),
        cost_estimate=pl.CostEstimate(flops=2 * share * plan.rank, bytes_accessed=4 * share, transcendentals=0),
        name="merge",
    )(*operands)


def on_device(shards, groups, base, narrow, wide, adapted_expert_index):
    rank = narrow.shape[3]
    rows, columns = narrow.shape[2], wide.shape[3]
    axes = ("shard", "group")
    narrow = jnp.swapaxes(narrow, 2, 3)

    if shards != 4 or groups != 4:
        both, w = select(narrow, wide, adapted_expert_index)
        n = lax.all_gather(both[:, :rows], "group", axis=1, tiled=True)
        w = lax.all_gather(w, axes, axis=1, tiled=True)
        whole = lambda s, g: 0
        n_pieces = [(0, 0, rows * groups, whole)]
        w_pieces = [(1, 0, columns * shards * groups, whole)]
        plan = Plan(rank, columns * shards * groups, 1, lambda s: 0, n_pieces, w_pieces)
        return merge(plan, base, [n, w])[0]

    def swap(x, axis, bit):
        return lax.ppermute(x, axis, [(i, i ^ bit) for i in range(4)])

    both, w = select(narrow, wide, adapted_expert_index)
    w3, w2, w1 = [swap(w, "shard", k) for k in (3, 2, 1)]
    width = base.shape[2]
    split = width * 11 // 16
    span = 2 * columns * groups
    near_half, far_half = lambda s: s // 2, lambda s: 1 - s // 2
    held = load(base, [(near_half, span, 0, width), (far_half, span, 0, split)], w1)
    line = pack([w2, w3], (held,))
    own_a = pack([both, swap(both, "group", 2), w1, swap(w1, "group", 2)], (line,))
    other_a = swap(own_a, "group", 1)
    line_x = swap(line, "group", 2)
    half = rows + columns
    n_pieces = [
        (i, first, rows, lambda s, g, m=m: g ^ m)
        for i, first, m in ((0, 0, 0), (0, half, 2), (1, 0, 1), (1, half, 3))
    ]

    def w_piece(i, first, k, m):
        return (i, first, columns, lambda s, g: ((s ^ k) % 2) * groups + (g ^ m))

    near, far = [], []
    for i, m in ((0, 0), (1, 1)):
        near += [w_piece(i, rows, 0, m), w_piece(i, half + rows, 0, m ^ 2)]
        near += [w_piece(i, 2 * half, 1, m), w_piece(i, 2 * half + columns, 1, m ^ 2)]
        for at, k in ((0, 2), (1, 3)):
            far += [w_piece(i + 2, at * columns, k, m), w_piece(i + 2, (at + 2) * columns, k, m ^ 2)]
    near_plan = Plan(rank, span, 2, near_half, n_pieces, near)
    far_plan = Plan(rank, span, 2, far_half, n_pieces, far)
    parts = [own_a, other_a]
    out, token = merge(near_plan, held, parts, after=(line,))
    own_b = pack([line, line_x], (token,))
    held = load(base, [(far_half, span, split, width)], own_b, held)
    return merge(far_plan, held, parts + [own_b, swap(own_b, "group", 1)], out)[0]


def solution(mesh):
    return jax.shard_map(
        functools.partial(on_device, mesh.shape["shard"], mesh.shape["group"]),
        mesh=mesh,
        in_specs=(
            P("parts", None, "shard", None),
            P("parts", None, ("shard", "group"), None),
            P("parts", None, None, ("shard", "group")),
            P("parts"),
        ),
        out_specs=P("parts", None, "shard", None),
        check_vma=False,
    )
```

```python
import functools
import typing

import jax
import jax.numpy as jnp
from jax import lax
from jax.experimental import pallas as pl
from jax.experimental.pallas import tpu as pltpu
from jax.sharding import PartitionSpec as P

adapter_scale = 0.5
out_slots = 3
tile_rows = 512
in_vmem = pl.BlockSpec(memory_space=pltpu.VMEM)
in_hbm = pl.BlockSpec(memory_space=pltpu.HBM)
anywhere = pl.BlockSpec(memory_space=pl.ANY)
vmem_limit = 24 * 2**20


def select_kernel(index_ref, narrow_ref, wide_ref, both_out, w_out, index, n_buf, w_buf, index_sem, sems):
    experts = index_ref.shape[0]
    rank = narrow_ref.shape[2]
    rows = n_buf.shape[2]
    index_copy = pltpu.make_async_copy(index_ref, index, index_sem)
    index_copy.start()
    index_copy.wait()
    n_copies, w_copies = [], []
    for e in range(experts):
        i = index[e]
        ranks = pl.ds(e * rank, rank)
        w_copies.append(pltpu.make_async_copy(wide_ref.at[i], w_buf.at[:, ranks], sems.at[e, 1]))
        n_copies.append(pltpu.make_async_copy(narrow_ref.at[i], n_buf.at[:, ranks], sems.at[e, 0]))
    for copy in w_copies + n_copies:
        copy.start()
    for copy in w_copies:
        copy.wait()
    for p in range(w_buf.shape[0]):
        w = w_buf[p].T
        w_out[p] = w
        both_out[p, rows:] = w
    for copy in n_copies:
        copy.wait()
    for p in range(n_buf.shape[0]):
        both_out[p, :rows] = (n_buf[p] * adapter_scale).T


def select(narrow, wide, index):
    experts = index.shape[0]
    _, projections, rank, rows = narrow.shape
    columns = wide.shape[3]
    deep = experts * rank
    return pl.pallas_call(
        select_kernel,
        out_shape=(
            jax.ShapeDtypeStruct((projections, rows + columns, deep), narrow.dtype),
            jax.ShapeDtypeStruct((projections, columns, deep), wide.dtype),
        ),
        in_specs=[in_hbm] * 3,
        out_specs=[in_vmem] * 2,
        scratch_shapes=[
            pltpu.SMEM((experts,), index.dtype),
            pltpu.VMEM((projections, deep, rows), narrow.dtype),
            pltpu.VMEM((projections, deep, columns), wide.dtype),
            pltpu.SemaphoreType.DMA,
            pltpu.SemaphoreType.DMA((experts, 2)),
        ],
        compiler_params=pltpu.CompilerParams(vmem_limit_bytes=vmem_limit),
        name="select",
    )(*[pltpu.with_memory_space_constraint(x, pltpu.HBM) for x in (index, narrow, wide)])


def load_kernel(blocks, base_ref, *refs):
    out_ref, sems = refs[-2:]
    s = lax.axis_index("shard")
    copies = []
    for n, (chunk, span, first, last) in enumerate(blocks):
        columns = pl.ds(pl.multiple_of(chunk(s) * span, span), span)
        rows = pl.ds(first, last - first)
        copies.append(
            pltpu.make_async_copy(base_ref.at[:, :, rows, columns], out_ref.at[:, :, rows, columns], sems.at[n])
        )
    for copy in copies:
        copy.start()
    for copy in copies:
        copy.wait()


def load(base, blocks, after, held=None):
    operands = [pltpu.with_memory_space_constraint(base, pltpu.HBM), after] + ([] if held is None else [held])
    return pl.pallas_call(
        functools.partial(load_kernel, blocks),
        out_shape=jax.ShapeDtypeStruct(base.shape, base.dtype),
        in_specs=[in_hbm, anywhere, in_vmem][: len(operands)],
        out_specs=in_vmem,
        scratch_shapes=[pltpu.SemaphoreType.DMA((len(blocks),))],
        input_output_aliases={} if held is None else {2: 0},
        compiler_params=pltpu.CompilerParams(vmem_limit_bytes=vmem_limit),
        cost_estimate=pl.CostEstimate(flops=0, bytes_accessed=2 * base.size, transcendentals=0),
        name="load",
    )(*operands)


def pack_kernel(count, *refs):
    out_ref = refs[-1]
    at = 0
    for ref in refs[:count]:
        rows = ref.shape[1]
        out_ref[:, at : at + rows] = ref[...]
        at += rows


def pack(blocks, after=()):
    projections, _, deep = blocks[0].shape
    rows = sum(x.shape[1] for x in blocks)
    return pl.pallas_call(
        functools.partial(pack_kernel, len(blocks)),
        out_shape=jax.ShapeDtypeStruct((projections, rows, deep), blocks[0].dtype),
        in_specs=[in_vmem] * len(blocks) + [anywhere] * len(after),
        out_specs=in_vmem,
        compiler_params=pltpu.CompilerParams(vmem_limit_bytes=vmem_limit),
        name="pack",
    )(*blocks, *after)


def merge_kernel(plan, held_ref, *refs):
    out_ref, token, n_all, w_all, out_buf, sems = refs[-6:]
    experts, projections, width, _ = held_ref.shape
    _, span, deep = w_all.shape
    m_step = tile_rows if width % tile_rows == 0 else width
    f_step = 256 if span % 256 == 0 else span
    steps = projections * experts
    s, g = lax.axis_index("shard"), lax.axis_index("group")
    lane_expert = lax.broadcasted_iota(jnp.int32, (m_step, deep), 1) // plan.rank

    def prepare(p):
        for i, first, rows, place in plan.n_pieces:
            at = pl.multiple_of(place(s, g) * rows, rows)
            n_all[p, pl.ds(at, rows), :] = refs[i][p, pl.ds(first, rows)]
        for i, first, rows, place in plan.w_pieces:
            at = pl.multiple_of(place(s, g) * rows, rows)
            w_all[p, pl.ds(at, rows), :] = refs[i][p, pl.ds(first, rows)]

    def merge_chunk(first_column):
        columns = pl.ds(first_column, span)

        def out_copies(step):
            p, e = step // experts, lax.rem(step, experts)
            slot = lax.rem(step, out_slots)
            return [
                pltpu.make_async_copy(
                    out_buf.at[slot, pl.ds(m, m_step)],
                    out_ref.at[e, p, pl.ds(m, m_step), columns],
                    sems.at[slot, m // m_step],
                )
                for m in range(0, width, m_step)
            ]

        def tile(step, _):
            p, e = step // experts, lax.rem(step, experts)
            slot = lax.rem(step, out_slots)
            pl.when(e == 0)(lambda: prepare(p))

            @pl.when(step >= out_slots)
            def _():
                for copy in out_copies(step - out_slots):
                    copy.wait()

            for copy, m in zip(out_copies(step), range(0, width, m_step)):
                n = n_all[p, m : m + m_step, :]
                n = jnp.where(lane_expert == e, n, jnp.zeros_like(n))
                for f in range(0, span, f_step):
                    delta = lax.dot_general(
                        n, w_all[p, f : f + f_step], (((1,), (1,)), ((), ())), preferred_element_type=jnp.float32
                    )
                    b = held_ref[e, p, m : m + m_step, first_column + f : first_column + f + f_step]
                    out_buf[slot, m : m + m_step, f : f + f_step] = (b.astype(jnp.float32) + delta).astype(out_buf.dtype)
                copy.start()
            return 0

        lax.fori_loop(0, steps, tile, 0)
        for step in range(max(0, steps - out_slots), steps):
            for copy in out_copies(jnp.int32(step)):
                copy.wait()

    for c in range(plan.chunks):
        pl.when(plan.chunk(s) == c)(functools.partial(merge_chunk, c * span))
    token[...] = jnp.zeros_like(token)


class Plan(typing.NamedTuple):
    rank: int
    span: int
    chunks: int
    chunk: typing.Callable
    n_pieces: list
    w_pieces: list


def merge(plan, held, parts, out=None, after=()):
    experts, projections, width, _ = held.shape
    deep = parts[0].shape[-1]
    share = projections * plan.span * experts * width
    extra = [*after] + ([] if out is None else [out])
    operands = [held, *parts, *extra]
    return pl.pallas_call(
        functools.partial(merge_kernel, plan),
        out_shape=[jax.ShapeDtypeStruct(held.shape, held.dtype), jax.ShapeDtypeStruct((8, 128), jnp.float32)],
        in_specs=[in_vmem] * (1 + len(parts)) + [anywhere] * len(extra),
        out_specs=[in_hbm, in_vmem],
        scratch_shapes=[
            pltpu.VMEM((projections, width, deep), held.dtype),
            pltpu.VMEM((projections, plan.span, deep), held.dtype),
            pltpu.VMEM((out_slots, width, plan.span), held.dtype),
            pltpu.SemaphoreType.DMA((out_slots, 2)),
        ],
        input_output_aliases={} if out is None else {len(operands) - 1: 0},
        compiler_params=pltpu.CompilerParams(vmem_limit_bytes=vmem_limit),
        cost_estimate=pl.CostEstimate(flops=2 * share * plan.rank, bytes_accessed=4 * share, transcendentals=0),
        name="merge",
    )(*operands)


def on_device(shards, groups, base, narrow, wide, adapted_expert_index):
    rank = narrow.shape[3]
    rows, columns = narrow.shape[2], wide.shape[3]
    axes = ("shard", "group")
    narrow = jnp.swapaxes(narrow, 2, 3)

    if shards != 4 or groups != 4:
        both, w = select(narrow, wide, adapted_expert_index)
        n = lax.all_gather(both[:, :rows], "group", axis=1, tiled=True)
        w = lax.all_gather(w, axes, axis=1, tiled=True)
        whole = lambda s, g: 0
        n_pieces = [(0, 0, rows * groups, whole)]
        w_pieces = [(1, 0, columns * shards * groups, whole)]
        plan = Plan(rank, columns * shards * groups, 1, lambda s: 0, n_pieces, w_pieces)
        return merge(plan, base, [n, w])[0]

    def swap(x, axis, bit):
        return lax.ppermute(x, axis, [(i, i ^ bit) for i in range(4)])

    both, w = select(narrow, wide, adapted_expert_index)
    w3, w2, w1 = [swap(w, "shard", k) for k in (3, 2, 1)]
    width = base.shape[2]
    split = width * 11 // 16
    span = 2 * columns * groups
    near_half, far_half = lambda s: s // 2, lambda s: 1 - s // 2
    held = load(base, [(near_half, span, 0, width), (far_half, span, 0, split)], w1)
    line = pack([w2, w3], (held,))
    own_a = pack([both, swap(both, "group", 2), w1, swap(w1, "group", 2)], (line,))
    other_a = swap(own_a, "group", 1)
    line_x = swap(line, "group", 2)
    half = rows + columns
    n_pieces = [
        (i, first, rows, lambda s, g, m=m: g ^ m)
        for i, first, m in ((0, 0, 0), (0, half, 2), (1, 0, 1), (1, half, 3))
    ]

    def w_piece(i, first, k, m):
        return (i, first, columns, lambda s, g: ((s ^ k) % 2) * groups + (g ^ m))

    near, far = [], []
    for i, m in ((0, 0), (1, 1)):
        near += [w_piece(i, rows, 0, m), w_piece(i, half + rows, 0, m ^ 2)]
        near += [w_piece(i, 2 * half, 1, m), w_piece(i, 2 * half + columns, 1, m ^ 2)]
        for at, k in ((0, 2), (1, 3)):
            far += [w_piece(i + 2, at * columns, k, m), w_piece(i + 2, (at + 2) * columns, k, m ^ 2)]
    near_plan = Plan(rank, span, 2, near_half, n_pieces, near)
    far_plan = Plan(rank, span, 2, far_half, n_pieces, far)
    parts = [own_a, other_a]
    out, token = merge(near_plan, held, parts, after=(line,))
    own_b = pack([line, line_x], (token,))
    held = load(base, [(far_half, span, split, width)], own_b, held)
    return merge(far_plan, held, parts + [own_b, swap(own_b, "group", 1)], out)[0]


def solution(mesh):
    return jax.shard_map(
        functools.partial(on_device, mesh.shape["shard"], mesh.shape["group"]),
        mesh=mesh,
        in_specs=(
            P("parts", None, "shard", None),
            P("parts", None, ("shard", "group"), None),
            P("parts", None, None, ("shard", "group")),
            P("parts"),
        ),
        out_specs=P("parts", None, "shard", None),
        check_vma=False,
    )
```

```python
import functools
import typing

import jax
import jax.numpy as jnp
from jax import lax
from jax.experimental import pallas as pl
from jax.experimental.pallas import tpu as pltpu
from jax.sharding import PartitionSpec as P

adapter_scale = 0.5
out_slots = 3
tile_rows = 512
in_vmem = pl.BlockSpec(memory_space=pltpu.VMEM)
in_hbm = pl.BlockSpec(memory_space=pltpu.HBM)
anywhere = pl.BlockSpec(memory_space=pl.ANY)
vmem_limit = 24 * 2**20


def select_kernel(index_ref, narrow_ref, wide_ref, both_out, w_out, index, n_buf, w_buf, index_sem, sems):
    experts = index_ref.shape[0]
    rank = narrow_ref.shape[2]
    rows = n_buf.shape[2]
    index_copy = pltpu.make_async_copy(index_ref, index, index_sem)
    index_copy.start()
    index_copy.wait()
    n_copies, w_copies = [], []
    for e in range(experts):
        i = index[e]
        ranks = pl.ds(e * rank, rank)
        w_copies.append(pltpu.make_async_copy(wide_ref.at[i], w_buf.at[:, ranks], sems.at[e, 1]))
        n_copies.append(pltpu.make_async_copy(narrow_ref.at[i], n_buf.at[:, ranks], sems.at[e, 0]))
    for copy in w_copies + n_copies:
        copy.start()
    for copy in w_copies:
        copy.wait()
    for p in range(w_buf.shape[0]):
        w = w_buf[p].T
        w_out[p] = w
        both_out[p, rows:] = w
    for copy in n_copies:
        copy.wait()
    for p in range(n_buf.shape[0]):
        both_out[p, :rows] = (n_buf[p] * adapter_scale).T


def select(narrow, wide, index):
    experts = index.shape[0]
    _, projections, rank, rows = narrow.shape
    columns = wide.shape[3]
    deep = experts * rank
    return pl.pallas_call(
        select_kernel,
        out_shape=(
            jax.ShapeDtypeStruct((projections, rows + columns, deep), narrow.dtype),
            jax.ShapeDtypeStruct((projections, columns, deep), wide.dtype),
        ),
        in_specs=[in_hbm] * 3,
        out_specs=[in_vmem] * 2,
        scratch_shapes=[
            pltpu.SMEM((experts,), index.dtype),
            pltpu.VMEM((projections, deep, rows), narrow.dtype),
            pltpu.VMEM((projections, deep, columns), wide.dtype),
            pltpu.SemaphoreType.DMA,
            pltpu.SemaphoreType.DMA((experts, 2)),
        ],
        compiler_params=pltpu.CompilerParams(vmem_limit_bytes=vmem_limit),
        name="select",
    )(*[pltpu.with_memory_space_constraint(x, pltpu.HBM) for x in (index, narrow, wide)])


def load_kernel(blocks, base_ref, *refs):
    out_ref, sems = refs[-2:]
    s = lax.axis_index("shard")
    copies = []
    for n, (chunk, span, first, last) in enumerate(blocks):
        columns = pl.ds(pl.multiple_of(chunk(s) * span, span), span)
        rows = pl.ds(first, last - first)
        copies.append(
            pltpu.make_async_copy(base_ref.at[:, :, rows, columns], out_ref.at[:, :, rows, columns], sems.at[n])
        )
    for copy in copies:
        copy.start()
    for copy in copies:
        copy.wait()


def load(base, blocks, after, held=None):
    operands = [pltpu.with_memory_space_constraint(base, pltpu.HBM), after] + ([] if held is None else [held])
    return pl.pallas_call(
        functools.partial(load_kernel, blocks),
        out_shape=jax.ShapeDtypeStruct(base.shape, base.dtype),
        in_specs=[in_hbm, anywhere, in_vmem][: len(operands)],
        out_specs=in_vmem,
        scratch_shapes=[pltpu.SemaphoreType.DMA((len(blocks),))],
        input_output_aliases={} if held is None else {2: 0},
        compiler_params=pltpu.CompilerParams(vmem_limit_bytes=vmem_limit),
        cost_estimate=pl.CostEstimate(flops=0, bytes_accessed=2 * base.size, transcendentals=0),
        name="load",
    )(*operands)


def pack_kernel(count, *refs):
    out_ref = refs[-1]
    at = 0
    for ref in refs[:count]:
        rows = ref.shape[1]
        out_ref[:, at : at + rows] = ref[...]
        at += rows


def pack(blocks, after=()):
    projections, _, deep = blocks[0].shape
    rows = sum(x.shape[1] for x in blocks)
    return pl.pallas_call(
        functools.partial(pack_kernel, len(blocks)),
        out_shape=jax.ShapeDtypeStruct((projections, rows, deep), blocks[0].dtype),
        in_specs=[in_vmem] * len(blocks) + [anywhere] * len(after),
        out_specs=in_vmem,
        compiler_params=pltpu.CompilerParams(vmem_limit_bytes=vmem_limit),
        name="pack",
    )(*blocks, *after)


def merge_kernel(plan, held_ref, *refs):
    out_ref, token, n_all, w_rows, w_all, out_buf, sems = refs[-7:]
    experts, projections, width, _ = held_ref.shape
    deep, span = w_all.shape
    m_step = tile_rows if width % tile_rows == 0 else width
    f_step = 256 if span % 256 == 0 else span
    steps = projections * experts
    s, g = lax.axis_index("shard"), lax.axis_index("group")
    lane_expert = lax.broadcasted_iota(jnp.int32, (width, deep), 1) // plan.rank

    def prepare(p):
        for i, first, rows, place in plan.n_pieces:
            at = pl.multiple_of(place(s, g) * rows, rows)
            n_all[pl.ds(at, rows), :] = refs[i][p, pl.ds(first, rows)]
        for i, first, rows, place in plan.w_pieces:
            at = pl.multiple_of(place(s, g) * rows, rows)
            w_rows[pl.ds(at, rows), :] = refs[i][p, pl.ds(first, rows)]
        for f in range(0, span, f_step):
            w_all[:, f : f + f_step] = w_rows[f : f + f_step].T

    def merge_chunk(first_column):
        columns = pl.ds(first_column, span)

        def out_copies(step):
            p, e = step // experts, lax.rem(step, experts)
            slot = lax.rem(step, out_slots)
            return [
                pltpu.make_async_copy(
                    out_buf.at[slot, pl.ds(m, m_step)],
                    out_ref.at[e, p, pl.ds(m, m_step), columns],
                    sems.at[slot, m // m_step],
                )
                for m in range(0, width, m_step)
            ]

        def tile(step, _):
            p, e = step // experts, lax.rem(step, experts)
            slot = lax.rem(step, out_slots)
            pl.when(e == 0)(lambda: prepare(p))

            @pl.when(step >= out_slots)
            def _():
                for copy in out_copies(step - out_slots):
                    copy.wait()

            n = n_all[...]
            n = jnp.where(lane_expert == e, n, jnp.zeros_like(n))
            for f in range(0, span, f_step):
                delta = jnp.dot(n, w_all[:, f : f + f_step], preferred_element_type=jnp.float32)
                b = held_ref[e, p, :, first_column + f : first_column + f + f_step].astype(jnp.float32)
                out_buf[slot, :, f : f + f_step] = (b + delta).astype(out_buf.dtype)
            for copy in out_copies(step):
                copy.start()
            return 0

        lax.fori_loop(0, steps, tile, 0)
        for step in range(max(0, steps - out_slots), steps):
            for copy in out_copies(jnp.int32(step)):
                copy.wait()

    for c in range(plan.chunks):
        pl.when(plan.chunk(s) == c)(functools.partial(merge_chunk, c * span))
    token[...] = jnp.zeros_like(token)


class Plan(typing.NamedTuple):
    rank: int
    span: int
    chunks: int
    chunk: typing.Callable
    n_pieces: list
    w_pieces: list


def merge(plan, held, parts, out=None, after=()):
    experts, projections, width, _ = held.shape
    deep = parts[0].shape[-1]
    share = projections * plan.span * experts * width
    extra = [*after] + ([] if out is None else [out])
    operands = [held, *parts, *extra]
    return pl.pallas_call(
        functools.partial(merge_kernel, plan),
        out_shape=[jax.ShapeDtypeStruct(held.shape, held.dtype), jax.ShapeDtypeStruct((8, 128), jnp.float32)],
        in_specs=[in_vmem] * (1 + len(parts)) + [anywhere] * len(extra),
        out_specs=[in_hbm, in_vmem],
        scratch_shapes=[
            pltpu.VMEM((width, deep), held.dtype),
            pltpu.VMEM((plan.span, deep), held.dtype),
            pltpu.VMEM((deep, plan.span), held.dtype),
            pltpu.VMEM((out_slots, width, plan.span), held.dtype),
            pltpu.SemaphoreType.DMA((out_slots, 2)),
        ],
        input_output_aliases={} if out is None else {len(operands) - 1: 0},
        compiler_params=pltpu.CompilerParams(vmem_limit_bytes=vmem_limit),
        cost_estimate=pl.CostEstimate(flops=2 * share * plan.rank, bytes_accessed=4 * share, transcendentals=0),
        name="merge",
    )(*operands)


def on_device(shards, groups, base, narrow, wide, adapted_expert_index):
    rank = narrow.shape[3]
    rows, columns = narrow.shape[2], wide.shape[3]
    axes = ("shard", "group")
    narrow = jnp.swapaxes(narrow, 2, 3)

    if shards != 4 or groups != 4:
        both, w = select(narrow, wide, adapted_expert_index)
        n = lax.all_gather(both[:, :rows], "group", axis=1, tiled=True)
        w = lax.all_gather(w, axes, axis=1, tiled=True)
        whole = lambda s, g: 0
        n_pieces = [(0, 0, rows * groups, whole)]
        w_pieces = [(1, 0, columns * shards * groups, whole)]
        plan = Plan(rank, columns * shards * groups, 1, lambda s: 0, n_pieces, w_pieces)
        return merge(plan, base, [n, w])[0]

    def swap(x, axis, bit):
        return lax.ppermute(x, axis, [(i, i ^ bit) for i in range(4)])

    both, w = select(narrow, wide, adapted_expert_index)
    w3, w2, w1 = [swap(w, "shard", k) for k in (3, 2, 1)]
    width = base.shape[2]
    split = width * 11 // 16
    span = 2 * columns * groups
    near_half, far_half = lambda s: s // 2, lambda s: 1 - s // 2
    held = load(base, [(near_half, span, 0, width), (far_half, span, 0, split)], w1)
    line = pack([w2, w3], (held,))
    own_a = pack([both, swap(both, "group", 2), w1, swap(w1, "group", 2)], (line,))
    other_a = swap(own_a, "group", 1)
    line_x = swap(line, "group", 2)
    half = rows + columns
    n_pieces = [
        (i, first, rows, lambda s, g, m=m: g ^ m)
        for i, first, m in ((0, 0, 0), (0, half, 2), (1, 0, 1), (1, half, 3))
    ]

    def w_piece(i, first, k, m):
        return (i, first, columns, lambda s, g: ((s ^ k) % 2) * groups + (g ^ m))

    near, far = [], []
    for i, m in ((0, 0), (1, 1)):
        near += [w_piece(i, rows, 0, m), w_piece(i, half + rows, 0, m ^ 2)]
        near += [w_piece(i, 2 * half, 1, m), w_piece(i, 2 * half + columns, 1, m ^ 2)]
        for at, k in ((0, 2), (1, 3)):
            far += [w_piece(i + 2, at * columns, k, m), w_piece(i + 2, (at + 2) * columns, k, m ^ 2)]
    near_plan = Plan(rank, span, 2, near_half, n_pieces, near)
    far_plan = Plan(rank, span, 2, far_half, n_pieces, far)
    parts = [own_a, other_a]
    out, token = merge(near_plan, held, parts, after=(line,))
    own_b = pack([line, line_x], (token,))
    held = load(base, [(far_half, span, split, width)], own_b, held)
    return merge(far_plan, held, parts + [own_b, swap(own_b, "group", 1)], out)[0]


def solution(mesh):
    return jax.shard_map(
        functools.partial(on_device, mesh.shape["shard"], mesh.shape["group"]),
        mesh=mesh,
        in_specs=(
            P("parts", None, "shard", None),
            P("parts", None, ("shard", "group"), None),
            P("parts", None, None, ("shard", "group")),
            P("parts"),
        ),
        out_specs=P("parts", None, "shard", None),
        check_vma=False,
    )
```

```python
import functools
import typing

import jax
import jax.numpy as jnp
from jax import lax
from jax.experimental import pallas as pl
from jax.experimental.pallas import tpu as pltpu
from jax.sharding import PartitionSpec as P

adapter_scale = 0.5
out_slots = 3
tile_rows = 256
in_vmem = pl.BlockSpec(memory_space=pltpu.VMEM)
in_hbm = pl.BlockSpec(memory_space=pltpu.HBM)
anywhere = pl.BlockSpec(memory_space=pl.ANY)
vmem_limit = 24 * 2**20


def select_kernel(index_ref, narrow_ref, wide_ref, both_out, w_out, index, n_buf, w_buf, index_sem, sems):
    experts = index_ref.shape[0]
    rank = narrow_ref.shape[2]
    rows = n_buf.shape[2]
    index_copy = pltpu.make_async_copy(index_ref, index, index_sem)
    index_copy.start()
    index_copy.wait()
    n_copies, w_copies = [], []
    for e in range(experts):
        i = index[e]
        ranks = pl.ds(e * rank, rank)
        w_copies.append(pltpu.make_async_copy(wide_ref.at[i], w_buf.at[:, ranks], sems.at[e, 1]))
        n_copies.append(pltpu.make_async_copy(narrow_ref.at[i], n_buf.at[:, ranks], sems.at[e, 0]))
    for copy in w_copies + n_copies:
        copy.start()
    for copy in w_copies:
        copy.wait()
    for p in range(w_buf.shape[0]):
        w = w_buf[p].T
        w_out[p] = w
        both_out[p, rows:] = w
    for copy in n_copies:
        copy.wait()
    for p in range(n_buf.shape[0]):
        both_out[p, :rows] = (n_buf[p] * adapter_scale).T


def select(narrow, wide, index):
    experts = index.shape[0]
    _, projections, rank, rows = narrow.shape
    columns = wide.shape[3]
    deep = experts * rank
    return pl.pallas_call(
        select_kernel,
        out_shape=(
            jax.ShapeDtypeStruct((projections, rows + columns, deep), narrow.dtype),
            jax.ShapeDtypeStruct((projections, columns, deep), wide.dtype),
        ),
        in_specs=[in_hbm] * 3,
        out_specs=[in_vmem] * 2,
        scratch_shapes=[
            pltpu.SMEM((experts,), index.dtype),
            pltpu.VMEM((projections, deep, rows), narrow.dtype),
            pltpu.VMEM((projections, deep, columns), wide.dtype),
            pltpu.SemaphoreType.DMA,
            pltpu.SemaphoreType.DMA((experts, 2)),
        ],
        compiler_params=pltpu.CompilerParams(vmem_limit_bytes=vmem_limit),
        name="select",
    )(*[pltpu.with_memory_space_constraint(x, pltpu.HBM) for x in (index, narrow, wide)])


def load_kernel(blocks, base_ref, *refs):
    out_ref, sems = refs[-2:]
    s = lax.axis_index("shard")
    copies = []
    for n, (chunk, span, first, last) in enumerate(blocks):
        columns = pl.ds(pl.multiple_of(chunk(s) * span, span), span)
        rows = pl.ds(first, last - first)
        copies.append(
            pltpu.make_async_copy(base_ref.at[:, :, rows, columns], out_ref.at[:, :, rows, columns], sems.at[n])
        )
    for copy in copies:
        copy.start()
    for copy in copies:
        copy.wait()


def load(base, blocks, after, held=None):
    operands = [pltpu.with_memory_space_constraint(base, pltpu.HBM), after] + ([] if held is None else [held])
    return pl.pallas_call(
        functools.partial(load_kernel, blocks),
        out_shape=jax.ShapeDtypeStruct(base.shape, base.dtype),
        in_specs=[in_hbm, anywhere, in_vmem][: len(operands)],
        out_specs=in_vmem,
        scratch_shapes=[pltpu.SemaphoreType.DMA((len(blocks),))],
        input_output_aliases={} if held is None else {2: 0},
        compiler_params=pltpu.CompilerParams(vmem_limit_bytes=vmem_limit),
        cost_estimate=pl.CostEstimate(flops=0, bytes_accessed=2 * base.size, transcendentals=0),
        name="load",
    )(*operands)


def pack_kernel(count, *refs):
    out_ref = refs[-1]
    at = 0
    for ref in refs[:count]:
        rows = ref.shape[1]
        out_ref[:, at : at + rows] = ref[...]
        at += rows


def pack(blocks, after=()):
    projections, _, deep = blocks[0].shape
    rows = sum(x.shape[1] for x in blocks)
    return pl.pallas_call(
        functools.partial(pack_kernel, len(blocks)),
        out_shape=jax.ShapeDtypeStruct((projections, rows, deep), blocks[0].dtype),
        in_specs=[in_vmem] * len(blocks) + [anywhere] * len(after),
        out_specs=in_vmem,
        compiler_params=pltpu.CompilerParams(vmem_limit_bytes=vmem_limit),
        name="pack",
    )(*blocks, *after)


def merge_kernel(plan, held_ref, *refs):
    out_ref, token, n_all, w_all, out_buf, sems = refs[-6:]
    experts, projections, width, _ = held_ref.shape
    _, span, deep = w_all.shape
    m_step = tile_rows if width % tile_rows == 0 else width
    f_step = 256 if span % 256 == 0 else span
    steps = projections * experts
    s, g = lax.axis_index("shard"), lax.axis_index("group")
    lane_expert = lax.broadcasted_iota(jnp.int32, (m_step, deep), 1) // plan.rank

    def prepare(p):
        for i, first, rows, place in plan.n_pieces:
            at = pl.multiple_of(place(s, g) * rows, rows)
            n_all[p, pl.ds(at, rows), :] = refs[i][p, pl.ds(first, rows)]
        for i, first, rows, place in plan.w_pieces:
            at = pl.multiple_of(place(s, g) * rows, rows)
            w_all[p, pl.ds(at, rows), :] = refs[i][p, pl.ds(first, rows)]

    def merge_chunk(first_column):
        columns = pl.ds(first_column, span)

        def out_copies(step):
            p, e = step // experts, lax.rem(step, experts)
            slot = lax.rem(step, out_slots)
            return [
                pltpu.make_async_copy(
                    out_buf.at[slot, pl.ds(m, m_step)],
                    out_ref.at[e, p, pl.ds(m, m_step), columns],
                    sems.at[slot, m // m_step],
                )
                for m in range(0, width, m_step)
            ]

        def tile(step, _):
            p, e = step // experts, lax.rem(step, experts)
            slot = lax.rem(step, out_slots)
            pl.when(e == 0)(lambda: prepare(p))

            @pl.when(step >= out_slots)
            def _():
                for copy in out_copies(step - out_slots):
                    copy.wait()

            for copy, m in zip(out_copies(step), range(0, width, m_step)):
                n = n_all[p, m : m + m_step, :]
                n = jnp.where(lane_expert == e, n, jnp.zeros_like(n))
                for f in range(0, span, f_step):
                    delta = lax.dot_general(
                        n, w_all[p, f : f + f_step], (((1,), (1,)), ((), ())), preferred_element_type=jnp.float32
                    )
                    b = held_ref[e, p, m : m + m_step, first_column + f : first_column + f + f_step]
                    out_buf[slot, m : m + m_step, f : f + f_step] = (b.astype(jnp.float32) + delta).astype(out_buf.dtype)
                copy.start()
            return 0

        lax.fori_loop(0, steps, tile, 0)
        for step in range(max(0, steps - out_slots), steps):
            for copy in out_copies(jnp.int32(step)):
                copy.wait()

    for c in range(plan.chunks):
        pl.when(plan.chunk(s) == c)(functools.partial(merge_chunk, c * span))
    token[...] = jnp.zeros_like(token)


class Plan(typing.NamedTuple):
    rank: int
    span: int
    chunks: int
    chunk: typing.Callable
    n_pieces: list
    w_pieces: list


def merge(plan, held, parts, out=None, after=()):
    experts, projections, width, _ = held.shape
    deep = parts[0].shape[-1]
    m_step = tile_rows if width % tile_rows == 0 else width
    share = projections * plan.span * experts * width
    extra = [*after] + ([] if out is None else [out])
    operands = [held, *parts, *extra]
    return pl.pallas_call(
        functools.partial(merge_kernel, plan),
        out_shape=[jax.ShapeDtypeStruct(held.shape, held.dtype), jax.ShapeDtypeStruct((8, 128), jnp.float32)],
        in_specs=[in_vmem] * (1 + len(parts)) + [anywhere] * len(extra),
        out_specs=[in_hbm, in_vmem],
        scratch_shapes=[
            pltpu.VMEM((projections, width, deep), held.dtype),
            pltpu.VMEM((projections, plan.span, deep), held.dtype),
            pltpu.VMEM((out_slots, width, plan.span), held.dtype),
            pltpu.SemaphoreType.DMA((out_slots, width // m_step)),
        ],
        input_output_aliases={} if out is None else {len(operands) - 1: 0},
        compiler_params=pltpu.CompilerParams(vmem_limit_bytes=vmem_limit),
        cost_estimate=pl.CostEstimate(flops=2 * share * plan.rank, bytes_accessed=4 * share, transcendentals=0),
        name="merge",
    )(*operands)


def on_device(shards, groups, base, narrow, wide, adapted_expert_index):
    rank = narrow.shape[3]
    rows, columns = narrow.shape[2], wide.shape[3]
    axes = ("shard", "group")
    narrow = jnp.swapaxes(narrow, 2, 3)

    if shards != 4 or groups != 4:
        both, w = select(narrow, wide, adapted_expert_index)
        n = lax.all_gather(both[:, :rows], "group", axis=1, tiled=True)
        w = lax.all_gather(w, axes, axis=1, tiled=True)
        whole = lambda s, g: 0
        n_pieces = [(0, 0, rows * groups, whole)]
        w_pieces = [(1, 0, columns * shards * groups, whole)]
        plan = Plan(rank, columns * shards * groups, 1, lambda s: 0, n_pieces, w_pieces)
        return merge(plan, base, [n, w])[0]

    def swap(x, axis, bit):
        return lax.ppermute(x, axis, [(i, i ^ bit) for i in range(4)])

    both, w = select(narrow, wide, adapted_expert_index)
    w3, w2, w1 = [swap(w, "shard", k) for k in (3, 2, 1)]
    width = base.shape[2]
    split = width * 11 // 16
    span = 2 * columns * groups
    near_half, far_half = lambda s: s // 2, lambda s: 1 - s // 2
    held = load(base, [(near_half, span, 0, width), (far_half, span, 0, split)], w1)
    line = pack([w2, w3], (held,))
    own_a = pack([both, swap(both, "group", 2), w1, swap(w1, "group", 2)], (line,))
    other_a = swap(own_a, "group", 1)
    line_x = swap(line, "group", 2)
    half = rows + columns
    n_pieces = [
        (i, first, rows, lambda s, g, m=m: g ^ m)
        for i, first, m in ((0, 0, 0), (0, half, 2), (1, 0, 1), (1, half, 3))
    ]

    def w_piece(i, first, k, m):
        return (i, first, columns, lambda s, g: ((s ^ k) % 2) * groups + (g ^ m))

    near, far = [], []
    for i, m in ((0, 0), (1, 1)):
        near += [w_piece(i, rows, 0, m), w_piece(i, half + rows, 0, m ^ 2)]
        near += [w_piece(i, 2 * half, 1, m), w_piece(i, 2 * half + columns, 1, m ^ 2)]
        for at, k in ((0, 2), (1, 3)):
            far += [w_piece(i + 2, at * columns, k, m), w_piece(i + 2, (at + 2) * columns, k, m ^ 2)]
    near_plan = Plan(rank, span, 2, near_half, n_pieces, near)
    far_plan = Plan(rank, span, 2, far_half, n_pieces, far)
    parts = [own_a, other_a]
    out, token = merge(near_plan, held, parts, after=(line,))
    own_b = pack([line, line_x], (token,))
    held = load(base, [(far_half, span, split, width)], own_b, held)
    return merge(far_plan, held, parts + [own_b, swap(own_b, "group", 1)], out)[0]


def solution(mesh):
    return jax.shard_map(
        functools.partial(on_device, mesh.shape["shard"], mesh.shape["group"]),
        mesh=mesh,
        in_specs=(
            P("parts", None, "shard", None),
            P("parts", None, ("shard", "group"), None),
            P("parts", None, None, ("shard", "group")),
            P("parts"),
        ),
        out_specs=P("parts", None, "shard", None),
        check_vma=False,
    )
```

```python
import functools
import typing

import jax
import jax.numpy as jnp
from jax import lax
from jax.experimental import pallas as pl
from jax.experimental.pallas import tpu as pltpu
from jax.sharding import PartitionSpec as P

adapter_scale = 0.5
out_slots = 3
tile_rows = 128
in_vmem = pl.BlockSpec(memory_space=pltpu.VMEM)
in_hbm = pl.BlockSpec(memory_space=pltpu.HBM)
anywhere = pl.BlockSpec(memory_space=pl.ANY)
vmem_limit = 24 * 2**20


def select_kernel(index_ref, narrow_ref, wide_ref, both_out, w_out, index, n_buf, w_buf, index_sem, sems):
    experts = index_ref.shape[0]
    rank = narrow_ref.shape[2]
    rows = n_buf.shape[2]
    index_copy = pltpu.make_async_copy(index_ref, index, index_sem)
    index_copy.start()
    index_copy.wait()
    n_copies, w_copies = [], []
    for e in range(experts):
        i = index[e]
        ranks = pl.ds(e * rank, rank)
        w_copies.append(pltpu.make_async_copy(wide_ref.at[i], w_buf.at[:, ranks], sems.at[e, 1]))
        n_copies.append(pltpu.make_async_copy(narrow_ref.at[i], n_buf.at[:, ranks], sems.at[e, 0]))
    for copy in w_copies + n_copies:
        copy.start()
    for copy in w_copies:
        copy.wait()
    for p in range(w_buf.shape[0]):
        w = w_buf[p].T
        w_out[p] = w
        both_out[p, rows:] = w
    for copy in n_copies:
        copy.wait()
    for p in range(n_buf.shape[0]):
        both_out[p, :rows] = (n_buf[p] * adapter_scale).T


def select(narrow, wide, index):
    experts = index.shape[0]
    _, projections, rank, rows = narrow.shape
    columns = wide.shape[3]
    deep = experts * rank
    return pl.pallas_call(
        select_kernel,
        out_shape=(
            jax.ShapeDtypeStruct((projections, rows + columns, deep), narrow.dtype),
            jax.ShapeDtypeStruct((projections, columns, deep), wide.dtype),
        ),
        in_specs=[in_hbm] * 3,
        out_specs=[in_vmem] * 2,
        scratch_shapes=[
            pltpu.SMEM((experts,), index.dtype),
            pltpu.VMEM((projections, deep, rows), narrow.dtype),
            pltpu.VMEM((projections, deep, columns), wide.dtype),
            pltpu.SemaphoreType.DMA,
            pltpu.SemaphoreType.DMA((experts, 2)),
        ],
        compiler_params=pltpu.CompilerParams(vmem_limit_bytes=vmem_limit),
        name="select",
    )(*[pltpu.with_memory_space_constraint(x, pltpu.HBM) for x in (index, narrow, wide)])


def load_kernel(blocks, base_ref, *refs):
    out_ref, sems = refs[-2:]
    s = lax.axis_index("shard")
    copies = []
    for n, (chunk, span, first, last) in enumerate(blocks):
        columns = pl.ds(pl.multiple_of(chunk(s) * span, span), span)
        rows = pl.ds(first, last - first)
        copies.append(
            pltpu.make_async_copy(base_ref.at[:, :, rows, columns], out_ref.at[:, :, rows, columns], sems.at[n])
        )
    for copy in copies:
        copy.start()
    for copy in copies:
        copy.wait()


def load(base, blocks, after, held=None):
    operands = [pltpu.with_memory_space_constraint(base, pltpu.HBM), after] + ([] if held is None else [held])
    return pl.pallas_call(
        functools.partial(load_kernel, blocks),
        out_shape=jax.ShapeDtypeStruct(base.shape, base.dtype),
        in_specs=[in_hbm, anywhere, in_vmem][: len(operands)],
        out_specs=in_vmem,
        scratch_shapes=[pltpu.SemaphoreType.DMA((len(blocks),))],
        input_output_aliases={} if held is None else {2: 0},
        compiler_params=pltpu.CompilerParams(vmem_limit_bytes=vmem_limit),
        cost_estimate=pl.CostEstimate(flops=0, bytes_accessed=2 * base.size, transcendentals=0),
        name="load",
    )(*operands)


def pack_kernel(count, *refs):
    out_ref = refs[-1]
    at = 0
    for ref in refs[:count]:
        rows = ref.shape[1]
        out_ref[:, at : at + rows] = ref[...]
        at += rows


def pack(blocks, after=()):
    projections, _, deep = blocks[0].shape
    rows = sum(x.shape[1] for x in blocks)
    return pl.pallas_call(
        functools.partial(pack_kernel, len(blocks)),
        out_shape=jax.ShapeDtypeStruct((projections, rows, deep), blocks[0].dtype),
        in_specs=[in_vmem] * len(blocks) + [anywhere] * len(after),
        out_specs=in_vmem,
        compiler_params=pltpu.CompilerParams(vmem_limit_bytes=vmem_limit),
        name="pack",
    )(*blocks, *after)


def merge_kernel(plan, held_ref, *refs):
    out_ref, token, n_all, w_all, out_buf, sems = refs[-6:]
    experts, projections, width, _ = held_ref.shape
    _, span, deep = w_all.shape
    m_step = tile_rows if width % tile_rows == 0 else width
    f_step = 256 if span % 256 == 0 else span
    steps = projections * experts
    s, g = lax.axis_index("shard"), lax.axis_index("group")
    lane_expert = lax.broadcasted_iota(jnp.int32, (m_step, deep), 1) // plan.rank

    def prepare(p):
        for i, first, rows, place in plan.n_pieces:
            at = pl.multiple_of(place(s, g) * rows, rows)
            n_all[p, pl.ds(at, rows), :] = refs[i][p, pl.ds(first, rows)]
        for i, first, rows, place in plan.w_pieces:
            at = pl.multiple_of(place(s, g) * rows, rows)
            w_all[p, pl.ds(at, rows), :] = refs[i][p, pl.ds(first, rows)]

    def merge_chunk(first_column):
        columns = pl.ds(first_column, span)

        def out_copies(step):
            p, e = step // experts, lax.rem(step, experts)
            slot = lax.rem(step, out_slots)
            return [
                pltpu.make_async_copy(
                    out_buf.at[slot, pl.ds(m, m_step)],
                    out_ref.at[e, p, pl.ds(m, m_step), columns],
                    sems.at[slot, m // m_step],
                )
                for m in range(0, width, m_step)
            ]

        def tile(step, _):
            p, e = step // experts, lax.rem(step, experts)
            slot = lax.rem(step, out_slots)
            pl.when(e == 0)(lambda: prepare(p))

            @pl.when(step >= out_slots)
            def _():
                for copy in out_copies(step - out_slots):
                    copy.wait()

            for copy, m in zip(out_copies(step), range(0, width, m_step)):
                n = n_all[p, m : m + m_step, :]
                n = jnp.where(lane_expert == e, n, jnp.zeros_like(n))
                for f in range(0, span, f_step):
                    delta = lax.dot_general(
                        n, w_all[p, f : f + f_step], (((1,), (1,)), ((), ())), preferred_element_type=jnp.float32
                    )
                    b = held_ref[e, p, m : m + m_step, first_column + f : first_column + f + f_step]
                    out_buf[slot, m : m + m_step, f : f + f_step] = (b.astype(jnp.float32) + delta).astype(out_buf.dtype)
                copy.start()
            return 0

        lax.fori_loop(0, steps, tile, 0)
        for step in range(max(0, steps - out_slots), steps):
            for copy in out_copies(jnp.int32(step)):
                copy.wait()

    for c in range(plan.chunks):
        pl.when(plan.chunk(s) == c)(functools.partial(merge_chunk, c * span))
    token[...] = jnp.zeros_like(token)


class Plan(typing.NamedTuple):
    rank: int
    span: int
    chunks: int
    chunk: typing.Callable
    n_pieces: list
    w_pieces: list


def merge(plan, held, parts, out=None, after=()):
    experts, projections, width, _ = held.shape
    deep = parts[0].shape[-1]
    m_step = tile_rows if width % tile_rows == 0 else width
    share = projections * plan.span * experts * width
    extra = [*after] + ([] if out is None else [out])
    operands = [held, *parts, *extra]
    return pl.pallas_call(
        functools.partial(merge_kernel, plan),
        out_shape=[jax.ShapeDtypeStruct(held.shape, held.dtype), jax.ShapeDtypeStruct((8, 128), jnp.float32)],
        in_specs=[in_vmem] * (1 + len(parts)) + [anywhere] * len(extra),
        out_specs=[in_hbm, in_vmem],
        scratch_shapes=[
            pltpu.VMEM((projections, width, deep), held.dtype),
            pltpu.VMEM((projections, plan.span, deep), held.dtype),
            pltpu.VMEM((out_slots, width, plan.span), held.dtype),
            pltpu.SemaphoreType.DMA((out_slots, width // m_step)),
        ],
        input_output_aliases={} if out is None else {len(operands) - 1: 0},
        compiler_params=pltpu.CompilerParams(vmem_limit_bytes=vmem_limit),
        cost_estimate=pl.CostEstimate(flops=2 * share * plan.rank, bytes_accessed=4 * share, transcendentals=0),
        name="merge",
    )(*operands)


def on_device(shards, groups, base, narrow, wide, adapted_expert_index):
    rank = narrow.shape[3]
    rows, columns = narrow.shape[2], wide.shape[3]
    axes = ("shard", "group")
    narrow = jnp.swapaxes(narrow, 2, 3)

    if shards != 4 or groups != 4:
        both, w = select(narrow, wide, adapted_expert_index)
        n = lax.all_gather(both[:, :rows], "group", axis=1, tiled=True)
        w = lax.all_gather(w, axes, axis=1, tiled=True)
        whole = lambda s, g: 0
        n_pieces = [(0, 0, rows * groups, whole)]
        w_pieces = [(1, 0, columns * shards * groups, whole)]
        plan = Plan(rank, columns * shards * groups, 1, lambda s: 0, n_pieces, w_pieces)
        return merge(plan, base, [n, w])[0]

    def swap(x, axis, bit):
        return lax.ppermute(x, axis, [(i, i ^ bit) for i in range(4)])

    both, w = select(narrow, wide, adapted_expert_index)
    w3, w2, w1 = [swap(w, "shard", k) for k in (3, 2, 1)]
    width = base.shape[2]
    split = width * 13 // 16
    span = 2 * columns * groups
    near_half, far_half = lambda s: s // 2, lambda s: 1 - s // 2
    held = load(base, [(near_half, span, 0, width), (far_half, span, 0, split)], w1)
    line = pack([w2, w3], (held,))
    own_a = pack([both, swap(both, "group", 2), w1, swap(w1, "group", 2)], (line,))
    other_a = swap(own_a, "group", 1)
    line_x = swap(line, "group", 2)
    half = rows + columns
    n_pieces = [
        (i, first, rows, lambda s, g, m=m: g ^ m)
        for i, first, m in ((0, 0, 0), (0, half, 2), (1, 0, 1), (1, half, 3))
    ]

    def w_piece(i, first, k, m):
        return (i, first, columns, lambda s, g: ((s ^ k) % 2) * groups + (g ^ m))

    near, far = [], []
    for i, m in ((0, 0), (1, 1)):
        near += [w_piece(i, rows, 0, m), w_piece(i, half + rows, 0, m ^ 2)]
        near += [w_piece(i, 2 * half, 1, m), w_piece(i, 2 * half + columns, 1, m ^ 2)]
        for at, k in ((0, 2), (1, 3)):
            far += [w_piece(i + 2, at * columns, k, m), w_piece(i + 2, (at + 2) * columns, k, m ^ 2)]
    near_plan = Plan(rank, span, 2, near_half, n_pieces, near)
    far_plan = Plan(rank, span, 2, far_half, n_pieces, far)
    parts = [own_a, other_a]
    out, token = merge(near_plan, held, parts, after=(line,))
    own_b = pack([line, line_x], (token,))
    held = load(base, [(far_half, span, split, width)], own_b, held)
    return merge(far_plan, held, parts + [own_b, swap(own_b, "group", 1)], out)[0]


def solution(mesh):
    return jax.shard_map(
        functools.partial(on_device, mesh.shape["shard"], mesh.shape["group"]),
        mesh=mesh,
        in_specs=(
            P("parts", None, "shard", None),
            P("parts", None, ("shard", "group"), None),
            P("parts", None, None, ("shard", "group")),
            P("parts"),
        ),
        out_specs=P("parts", None, "shard", None),
        check_vma=False,
    )
```

```python
import functools
import typing

import jax
import jax.numpy as jnp
from jax import lax
from jax.experimental import pallas as pl
from jax.experimental.pallas import tpu as pltpu
from jax.sharding import PartitionSpec as P

adapter_scale = 0.5
out_slots = 6
tile_rows = 256
in_vmem = pl.BlockSpec(memory_space=pltpu.VMEM)
in_hbm = pl.BlockSpec(memory_space=pltpu.HBM)
anywhere = pl.BlockSpec(memory_space=pl.ANY)
vmem_limit = 24 * 2**20


def select_kernel(index_ref, narrow_ref, wide_ref, both_out, w_out, index, n_buf, w_buf, index_sem, sems):
    experts = index_ref.shape[0]
    rank = narrow_ref.shape[2]
    rows = n_buf.shape[2]
    index_copy = pltpu.make_async_copy(index_ref, index, index_sem)
    index_copy.start()
    index_copy.wait()
    n_copies, w_copies = [], []
    for e in range(experts):
        i = index[e]
        ranks = pl.ds(e * rank, rank)
        w_copies.append(pltpu.make_async_copy(wide_ref.at[i], w_buf.at[:, ranks], sems.at[e, 1]))
        n_copies.append(pltpu.make_async_copy(narrow_ref.at[i], n_buf.at[:, ranks], sems.at[e, 0]))
    for copy in w_copies + n_copies:
        copy.start()
    for copy in w_copies:
        copy.wait()
    for p in range(w_buf.shape[0]):
        w = w_buf[p].T
        w_out[p] = w
        both_out[p, rows:] = w
    for copy in n_copies:
        copy.wait()
    for p in range(n_buf.shape[0]):
        both_out[p, :rows] = (n_buf[p] * adapter_scale).T


def select(narrow, wide, index):
    experts = index.shape[0]
    _, projections, rank, rows = narrow.shape
    columns = wide.shape[3]
    deep = experts * rank
    return pl.pallas_call(
        select_kernel,
        out_shape=(
            jax.ShapeDtypeStruct((projections, rows + columns, deep), narrow.dtype),
            jax.ShapeDtypeStruct((projections, columns, deep), wide.dtype),
        ),
        in_specs=[in_hbm] * 3,
        out_specs=[in_vmem] * 2,
        scratch_shapes=[
            pltpu.SMEM((experts,), index.dtype),
            pltpu.VMEM((projections, deep, rows), narrow.dtype),
            pltpu.VMEM((projections, deep, columns), wide.dtype),
            pltpu.SemaphoreType.DMA,
            pltpu.SemaphoreType.DMA((experts, 2)),
        ],
        compiler_params=pltpu.CompilerParams(vmem_limit_bytes=vmem_limit),
        name="select",
    )(*[pltpu.with_memory_space_constraint(x, pltpu.HBM) for x in (index, narrow, wide)])


def load_kernel(blocks, base_ref, *refs):
    out_ref, sems = refs[-2:]
    s = lax.axis_index("shard")
    copies = []
    for n, (chunk, span, first, last) in enumerate(blocks):
        columns = pl.ds(pl.multiple_of(chunk(s) * span, span), span)
        rows = pl.ds(first, last - first)
        copies.append(
            pltpu.make_async_copy(base_ref.at[:, :, rows, columns], out_ref.at[:, :, rows, columns], sems.at[n])
        )
    for copy in copies:
        copy.start()
    for copy in copies:
        copy.wait()


def load(base, blocks, after, held=None):
    operands = [pltpu.with_memory_space_constraint(base, pltpu.HBM), after] + ([] if held is None else [held])
    return pl.pallas_call(
        functools.partial(load_kernel, blocks),
        out_shape=jax.ShapeDtypeStruct(base.shape, base.dtype),
        in_specs=[in_hbm, anywhere, in_vmem][: len(operands)],
        out_specs=in_vmem,
        scratch_shapes=[pltpu.SemaphoreType.DMA((len(blocks),))],
        input_output_aliases={} if held is None else {2: 0},
        compiler_params=pltpu.CompilerParams(vmem_limit_bytes=vmem_limit),
        cost_estimate=pl.CostEstimate(flops=0, bytes_accessed=2 * base.size, transcendentals=0),
        name="load",
    )(*operands)


def pack_kernel(count, *refs):
    out_ref = refs[-1]
    at = 0
    for ref in refs[:count]:
        rows = ref.shape[1]
        out_ref[:, at : at + rows] = ref[...]
        at += rows


def pack(blocks, after=()):
    projections, _, deep = blocks[0].shape
    rows = sum(x.shape[1] for x in blocks)
    return pl.pallas_call(
        functools.partial(pack_kernel, len(blocks)),
        out_shape=jax.ShapeDtypeStruct((projections, rows, deep), blocks[0].dtype),
        in_specs=[in_vmem] * len(blocks) + [anywhere] * len(after),
        out_specs=in_vmem,
        compiler_params=pltpu.CompilerParams(vmem_limit_bytes=vmem_limit),
        name="pack",
    )(*blocks, *after)


def merge_kernel(plan, held_ref, *refs):
    out_ref, token, n_all, w_all, out_buf, sems = refs[-6:]
    experts, projections, width, _ = held_ref.shape
    _, span, deep = w_all.shape
    m_step = tile_rows if width % tile_rows == 0 else width
    f_step = 256 if span % 256 == 0 else span
    steps = projections * experts
    s, g = lax.axis_index("shard"), lax.axis_index("group")
    lane_expert = lax.broadcasted_iota(jnp.int32, (m_step, deep), 1) // plan.rank

    def prepare(p):
        for i, first, rows, place in plan.n_pieces:
            at = pl.multiple_of(place(s, g) * rows, rows)
            n_all[p, pl.ds(at, rows), :] = refs[i][p, pl.ds(first, rows)]
        for i, first, rows, place in plan.w_pieces:
            at = pl.multiple_of(place(s, g) * rows, rows)
            w_all[p, pl.ds(at, rows), :] = refs[i][p, pl.ds(first, rows)]

    def merge_chunk(first_column):
        columns = pl.ds(first_column, span)

        def out_copies(step):
            p, e = step // experts, lax.rem(step, experts)
            slot = lax.rem(step, out_slots)
            return [
                pltpu.make_async_copy(
                    out_buf.at[slot, pl.ds(m, m_step)],
                    out_ref.at[e, p, pl.ds(m, m_step), columns],
                    sems.at[slot, m // m_step],
                )
                for m in range(0, width, m_step)
            ]

        def tile(step, _):
            p, e = step // experts, lax.rem(step, experts)
            slot = lax.rem(step, out_slots)
            pl.when(e == 0)(lambda: prepare(p))

            @pl.when(step >= out_slots)
            def _():
                for copy in out_copies(step - out_slots):
                    copy.wait()

            for copy, m in zip(out_copies(step), range(0, width, m_step)):
                n = n_all[p, m : m + m_step, :]
                n = jnp.where(lane_expert == e, n, jnp.zeros_like(n))
                for f in range(0, span, f_step):
                    delta = lax.dot_general(
                        n, w_all[p, f : f + f_step], (((1,), (1,)), ((), ())), preferred_element_type=jnp.float32
                    )
                    b = held_ref[e, p, m : m + m_step, first_column + f : first_column + f + f_step]
                    out_buf[slot, m : m + m_step, f : f + f_step] = (b.astype(jnp.float32) + delta).astype(out_buf.dtype)
                copy.start()
            return 0

        lax.fori_loop(0, steps, tile, 0)
        for step in range(max(0, steps - out_slots), steps):
            for copy in out_copies(jnp.int32(step)):
                copy.wait()

    for c in range(plan.chunks):
        pl.when(plan.chunk(s) == c)(functools.partial(merge_chunk, c * span))
    token[...] = jnp.zeros_like(token)


class Plan(typing.NamedTuple):
    rank: int
    span: int
    chunks: int
    chunk: typing.Callable
    n_pieces: list
    w_pieces: list


def merge(plan, held, parts, out=None, after=()):
    experts, projections, width, _ = held.shape
    deep = parts[0].shape[-1]
    m_step = tile_rows if width % tile_rows == 0 else width
    share = projections * plan.span * experts * width
    extra = [*after] + ([] if out is None else [out])
    operands = [held, *parts, *extra]
    return pl.pallas_call(
        functools.partial(merge_kernel, plan),
        out_shape=[jax.ShapeDtypeStruct(held.shape, held.dtype), jax.ShapeDtypeStruct((8, 128), jnp.float32)],
        in_specs=[in_vmem] * (1 + len(parts)) + [anywhere] * len(extra),
        out_specs=[in_hbm, in_vmem],
        scratch_shapes=[
            pltpu.VMEM((projections, width, deep), held.dtype),
            pltpu.VMEM((projections, plan.span, deep), held.dtype),
            pltpu.VMEM((out_slots, width, plan.span), held.dtype),
            pltpu.SemaphoreType.DMA((out_slots, width // m_step)),
        ],
        input_output_aliases={} if out is None else {len(operands) - 1: 0},
        compiler_params=pltpu.CompilerParams(vmem_limit_bytes=vmem_limit),
        cost_estimate=pl.CostEstimate(flops=2 * share * plan.rank, bytes_accessed=4 * share, transcendentals=0),
        name="merge",
    )(*operands)


def on_device(shards, groups, base, narrow, wide, adapted_expert_index):
    rank = narrow.shape[3]
    rows, columns = narrow.shape[2], wide.shape[3]
    axes = ("shard", "group")
    narrow = jnp.swapaxes(narrow, 2, 3)

    if shards != 4 or groups != 4:
        both, w = select(narrow, wide, adapted_expert_index)
        n = lax.all_gather(both[:, :rows], "group", axis=1, tiled=True)
        w = lax.all_gather(w, axes, axis=1, tiled=True)
        whole = lambda s, g: 0
        n_pieces = [(0, 0, rows * groups, whole)]
        w_pieces = [(1, 0, columns * shards * groups, whole)]
        plan = Plan(rank, columns * shards * groups, 1, lambda s: 0, n_pieces, w_pieces)
        return merge(plan, base, [n, w])[0]

    def swap(x, axis, bit):
        return lax.ppermute(x, axis, [(i, i ^ bit) for i in range(4)])

    both, w = select(narrow, wide, adapted_expert_index)
    w3, w2, w1 = [swap(w, "shard", k) for k in (3, 2, 1)]
    width = base.shape[2]
    split = width * 13 // 16
    span = 2 * columns * groups
    near_half, far_half = lambda s: s // 2, lambda s: 1 - s // 2
    held = load(base, [(near_half, span, 0, width), (far_half, span, 0, split)], w1)
    line = pack([w2, w3], (held,))
    own_a = pack([both, swap(both, "group", 2), w1, swap(w1, "group", 2)], (line,))
    other_a = swap(own_a, "group", 1)
    line_x = swap(line, "group", 2)
    half = rows + columns
    n_pieces = [
        (i, first, rows, lambda s, g, m=m: g ^ m)
        for i, first, m in ((0, 0, 0), (0, half, 2), (1, 0, 1), (1, half, 3))
    ]

    def w_piece(i, first, k, m):
        return (i, first, columns, lambda s, g: ((s ^ k) % 2) * groups + (g ^ m))

    near, far = [], []
    for i, m in ((0, 0), (1, 1)):
        near += [w_piece(i, rows, 0, m), w_piece(i, half + rows, 0, m ^ 2)]
        near += [w_piece(i, 2 * half, 1, m), w_piece(i, 2 * half + columns, 1, m ^ 2)]
        for at, k in ((0, 2), (1, 3)):
            far += [w_piece(i + 2, at * columns, k, m), w_piece(i + 2, (at + 2) * columns, k, m ^ 2)]
    near_plan = Plan(rank, span, 2, near_half, n_pieces, near)
    far_plan = Plan(rank, span, 2, far_half, n_pieces, far)
    parts = [own_a, other_a]
    out, token = merge(near_plan, held, parts, after=(line,))
    own_b = pack([line, line_x], (token,))
    held = load(base, [(far_half, span, split, width)], own_b, held)
    return merge(far_plan, held, parts + [own_b, swap(own_b, "group", 1)], out)[0]


def solution(mesh):
    return jax.shard_map(
        functools.partial(on_device, mesh.shape["shard"], mesh.shape["group"]),
        mesh=mesh,
        in_specs=(
            P("parts", None, "shard", None),
            P("parts", None, ("shard", "group"), None),
            P("parts", None, None, ("shard", "group")),
            P("parts"),
        ),
        out_specs=P("parts", None, "shard", None),
        check_vma=False,
    )
```

```python
import functools
import typing

import jax
import jax.numpy as jnp
from jax import lax
from jax.experimental import pallas as pl
from jax.experimental.pallas import tpu as pltpu
from jax.sharding import PartitionSpec as P

adapter_scale = 0.5
out_slots = 3
tile_rows = 256
in_vmem = pl.BlockSpec(memory_space=pltpu.VMEM)
in_hbm = pl.BlockSpec(memory_space=pltpu.HBM)
anywhere = pl.BlockSpec(memory_space=pl.ANY)
vmem_limit = 24 * 2**20


def select_kernel(index_ref, narrow_ref, wide_ref, both_out, w_out, index, n_buf, w_buf, index_sem, sems):
    experts = index_ref.shape[0]
    rank = narrow_ref.shape[2]
    rows = n_buf.shape[2]
    index_copy = pltpu.make_async_copy(index_ref, index, index_sem)
    index_copy.start()
    index_copy.wait()
    n_copies, w_copies = [], []
    for e in range(experts):
        i = index[e]
        ranks = pl.ds(e * rank, rank)
        w_copies.append(pltpu.make_async_copy(wide_ref.at[i], w_buf.at[:, ranks], sems.at[e, 1]))
        n_copies.append(pltpu.make_async_copy(narrow_ref.at[i], n_buf.at[:, ranks], sems.at[e, 0]))
    for copy in w_copies + n_copies:
        copy.start()
    for copy in w_copies:
        copy.wait()
    for p in range(w_buf.shape[0]):
        w = w_buf[p].T
        w_out[p] = w
        both_out[p, rows:] = w
    for copy in n_copies:
        copy.wait()
    for p in range(n_buf.shape[0]):
        both_out[p, :rows] = (n_buf[p] * adapter_scale).T


def select(narrow, wide, index):
    experts = index.shape[0]
    _, projections, rank, rows = narrow.shape
    columns = wide.shape[3]
    deep = experts * rank
    return pl.pallas_call(
        select_kernel,
        out_shape=(
            jax.ShapeDtypeStruct((projections, rows + columns, deep), narrow.dtype),
            jax.ShapeDtypeStruct((projections, columns, deep), wide.dtype),
        ),
        in_specs=[in_hbm] * 3,
        out_specs=[in_vmem] * 2,
        scratch_shapes=[
            pltpu.SMEM((experts,), index.dtype),
            pltpu.VMEM((projections, deep, rows), narrow.dtype),
            pltpu.VMEM((projections, deep, columns), wide.dtype),
            pltpu.SemaphoreType.DMA,
            pltpu.SemaphoreType.DMA((experts, 2)),
        ],
        compiler_params=pltpu.CompilerParams(vmem_limit_bytes=vmem_limit),
        name="select",
    )(*[pltpu.with_memory_space_constraint(x, pltpu.HBM) for x in (index, narrow, wide)])


def load_kernel(blocks, base_ref, *refs):
    out_ref, sems = refs[-2:]
    s = lax.axis_index("shard")
    copies = []
    for n, (chunk, span, first, last) in enumerate(blocks):
        columns = pl.ds(pl.multiple_of(chunk(s) * span, span), span)
        rows = pl.ds(first, last - first)
        copies.append(
            pltpu.make_async_copy(base_ref.at[:, :, rows, columns], out_ref.at[:, :, rows, columns], sems.at[n])
        )
    for copy in copies:
        copy.start()
    for copy in copies:
        copy.wait()


def load(base, blocks, after, held=None):
    operands = [pltpu.with_memory_space_constraint(base, pltpu.HBM), after] + ([] if held is None else [held])
    return pl.pallas_call(
        functools.partial(load_kernel, blocks),
        out_shape=jax.ShapeDtypeStruct(base.shape, base.dtype),
        in_specs=[in_hbm, anywhere, in_vmem][: len(operands)],
        out_specs=in_vmem,
        scratch_shapes=[pltpu.SemaphoreType.DMA((len(blocks),))],
        input_output_aliases={} if held is None else {2: 0},
        compiler_params=pltpu.CompilerParams(vmem_limit_bytes=vmem_limit),
        cost_estimate=pl.CostEstimate(flops=0, bytes_accessed=2 * base.size, transcendentals=0),
        name="load",
    )(*operands)


def pack_kernel(count, *refs):
    out_ref = refs[-1]
    at = 0
    for ref in refs[:count]:
        rows = ref.shape[1]
        out_ref[:, at : at + rows] = ref[...]
        at += rows


def pack(blocks, after=()):
    projections, _, deep = blocks[0].shape
    rows = sum(x.shape[1] for x in blocks)
    return pl.pallas_call(
        functools.partial(pack_kernel, len(blocks)),
        out_shape=jax.ShapeDtypeStruct((projections, rows, deep), blocks[0].dtype),
        in_specs=[in_vmem] * len(blocks) + [anywhere] * len(after),
        out_specs=in_vmem,
        compiler_params=pltpu.CompilerParams(vmem_limit_bytes=vmem_limit),
        name="pack",
    )(*blocks, *after)


def merge_kernel(plan, held_ref, *refs):
    out_ref, token, n_all, w_all, out_buf, sems = refs[-6:]
    experts, projections, width, _ = held_ref.shape
    _, span, deep = w_all.shape
    m_step = tile_rows if width % tile_rows == 0 else width
    f_step = 256 if span % 256 == 0 else span
    steps = projections * experts
    s, g = lax.axis_index("shard"), lax.axis_index("group")
    lane_expert = lax.broadcasted_iota(jnp.int32, (m_step, deep), 1) // plan.rank

    def prepare(p):
        for i, first, rows, place in plan.n_pieces:
            at = pl.multiple_of(place(s, g) * rows, rows)
            n_all[p, pl.ds(at, rows), :] = refs[i][p, pl.ds(first, rows)]
        for i, first, rows, place in plan.w_pieces:
            at = pl.multiple_of(place(s, g) * rows, rows)
            w_all[p, pl.ds(at, rows), :] = refs[i][p, pl.ds(first, rows)]

    def merge_chunk(first_column):
        columns = pl.ds(first_column, span)

        def out_copies(step):
            p, e = step // experts, lax.rem(step, experts)
            slot = lax.rem(step, out_slots)
            return [
                pltpu.make_async_copy(
                    out_buf.at[slot, pl.ds(m, m_step)],
                    out_ref.at[e, p, pl.ds(m, m_step), columns],
                    sems.at[slot, m // m_step],
                )
                for m in range(0, width, m_step)
            ]

        def tile(step, _):
            p, e = step // experts, lax.rem(step, experts)
            slot = lax.rem(step, out_slots)
            pl.when(e == 0)(lambda: prepare(p))

            @pl.when(step >= out_slots)
            def _():
                for copy in out_copies(step - out_slots):
                    copy.wait()

            for copy, m in zip(out_copies(step), range(0, width, m_step)):
                n = n_all[p, m : m + m_step, :]
                n = jnp.where(lane_expert == e, n, jnp.zeros_like(n))
                for f in range(0, span, f_step):
                    delta = lax.dot_general(
                        n, w_all[p, f : f + f_step], (((1,), (1,)), ((), ())), preferred_element_type=jnp.float32
                    )
                    b = held_ref[e, p, m : m + m_step, first_column + f : first_column + f + f_step]
                    out_buf[slot, m : m + m_step, f : f + f_step] = (b.astype(jnp.float32) + delta).astype(out_buf.dtype)
                copy.start()
            return 0

        lax.fori_loop(0, steps, tile, 0)
        for step in range(max(0, steps - out_slots), steps):
            for copy in out_copies(jnp.int32(step)):
                copy.wait()

    for c in range(plan.chunks):
        pl.when(plan.chunk(s) == c)(functools.partial(merge_chunk, c * span))
    token[...] = jnp.zeros_like(token)


class Plan(typing.NamedTuple):
    rank: int
    span: int
    chunks: int
    chunk: typing.Callable
    n_pieces: list
    w_pieces: list


def merge(plan, held, parts, out=None, after=()):
    experts, projections, width, _ = held.shape
    deep = parts[0].shape[-1]
    m_step = tile_rows if width % tile_rows == 0 else width
    share = projections * plan.span * experts * width
    extra = [*after] + ([] if out is None else [out])
    operands = [held, *parts, *extra]
    return pl.pallas_call(
        functools.partial(merge_kernel, plan),
        out_shape=[jax.ShapeDtypeStruct(held.shape, held.dtype), jax.ShapeDtypeStruct((8, 128), jnp.float32)],
        in_specs=[in_vmem] * (1 + len(parts)) + [anywhere] * len(extra),
        out_specs=[in_hbm, in_vmem],
        scratch_shapes=[
            pltpu.VMEM((projections, width, deep), held.dtype),
            pltpu.VMEM((projections, plan.span, deep), held.dtype),
            pltpu.VMEM((out_slots, width, plan.span), held.dtype),
            pltpu.SemaphoreType.DMA((out_slots, width // m_step)),
        ],
        input_output_aliases={} if out is None else {len(operands) - 1: 0},
        compiler_params=pltpu.CompilerParams(vmem_limit_bytes=vmem_limit),
        cost_estimate=pl.CostEstimate(flops=2 * share * plan.rank, bytes_accessed=4 * share, transcendentals=0),
        name="merge",
    )(*operands)


def on_device(shards, groups, base, narrow, wide, adapted_expert_index):
    rank = narrow.shape[3]
    rows, columns = narrow.shape[2], wide.shape[3]
    axes = ("shard", "group")
    narrow = jnp.swapaxes(narrow, 2, 3)

    if shards != 4 or groups != 4:
        both, w = select(narrow, wide, adapted_expert_index)
        n = lax.all_gather(both[:, :rows], "group", axis=1, tiled=True)
        w = lax.all_gather(w, axes, axis=1, tiled=True)
        whole = lambda s, g: 0
        n_pieces = [(0, 0, rows * groups, whole)]
        w_pieces = [(1, 0, columns * shards * groups, whole)]
        plan = Plan(rank, columns * shards * groups, 1, lambda s: 0, n_pieces, w_pieces)
        return merge(plan, base, [n, w])[0]

    def swap(x, axis, bit):
        return lax.ppermute(x, axis, [(i, i ^ bit) for i in range(4)])

    both, w = select(narrow, wide, adapted_expert_index)
    w3, w2, w1 = [swap(w, "shard", k) for k in (3, 2, 1)]
    width = base.shape[2]
    split = width * 13 // 16
    span = 2 * columns * groups
    near_half, far_half = lambda s: s // 2, lambda s: 1 - s // 2
    held = load(base, [(near_half, span, 0, width), (far_half, span, 0, split)], w1)
    line = pack([w2, w3], (held,))
    own_a = pack([both, swap(both, "group", 2), w1, swap(w1, "group", 2)], (line,))
    other_a = swap(own_a, "group", 1)
    line_x = swap(line, "group", 2)
    half = rows + columns
    n_pieces = [
        (i, first, rows, lambda s, g, m=m: g ^ m)
        for i, first, m in ((0, 0, 0), (0, half, 2), (1, 0, 1), (1, half, 3))
    ]

    def w_piece(i, first, k, m):
        return (i, first, columns, lambda s, g: ((s ^ k) % 2) * groups + (g ^ m))

    near, far = [], []
    for i, m in ((0, 0), (1, 1)):
        near += [w_piece(i, rows, 0, m), w_piece(i, half + rows, 0, m ^ 2)]
        near += [w_piece(i, 2 * half, 1, m), w_piece(i, 2 * half + columns, 1, m ^ 2)]
        for at, k in ((0, 2), (1, 3)):
            far += [w_piece(i + 2, at * columns, k, m), w_piece(i + 2, (at + 2) * columns, k, m ^ 2)]
    near_plan = Plan(rank, span, 2, near_half, n_pieces, near)
    far_plan = Plan(rank, span, 2, far_half, n_pieces, far)
    parts = [own_a, other_a]
    out, token = merge(near_plan, held, parts, after=(line,))
    own_b = pack([line, line_x], (token,))
    held = load(base, [(far_half, span, split, width)], own_b, held)
    return merge(far_plan, held, parts + [own_b, swap(own_b, "group", 1)], out)[0]


def solution(mesh):
    return jax.shard_map(
        functools.partial(on_device, mesh.shape["shard"], mesh.shape["group"]),
        mesh=mesh,
        in_specs=(
            P("parts", None, "shard", None),
            P("parts", None, ("shard", "group"), None),
            P("parts", None, None, ("shard", "group")),
            P("parts"),
        ),
        out_specs=P("parts", None, "shard", None),
        check_vma=False,
    )
```

```python
import functools
import typing

import jax
import jax.numpy as jnp
from jax import lax
from jax.experimental import pallas as pl
from jax.experimental.pallas import tpu as pltpu
from jax.sharding import PartitionSpec as P

adapter_scale = 0.5
out_slots = 3
tile_rows = 256
in_vmem = pl.BlockSpec(memory_space=pltpu.VMEM)
in_hbm = pl.BlockSpec(memory_space=pltpu.HBM)
anywhere = pl.BlockSpec(memory_space=pl.ANY)
vmem_limit = 24 * 2**20


def select_kernel(index_ref, narrow_ref, wide_ref, both_out, w_out, index, n_buf, w_buf, index_sem, sems):
    experts = index_ref.shape[0]
    rank = narrow_ref.shape[2]
    rows = n_buf.shape[2]
    index_copy = pltpu.make_async_copy(index_ref, index, index_sem)
    index_copy.start()
    index_copy.wait()
    n_copies, w_copies = [], []
    for e in range(experts):
        i = index[e]
        ranks = pl.ds(e * rank, rank)
        w_copies.append(pltpu.make_async_copy(wide_ref.at[i], w_buf.at[:, ranks], sems.at[e, 1]))
        n_copies.append(pltpu.make_async_copy(narrow_ref.at[i], n_buf.at[:, ranks], sems.at[e, 0]))
    for copy in w_copies + n_copies:
        copy.start()
    for copy in w_copies:
        copy.wait()
    for p in range(w_buf.shape[0]):
        w = w_buf[p].T
        w_out[p] = w
        both_out[p, rows:] = w
    for copy in n_copies:
        copy.wait()
    for p in range(n_buf.shape[0]):
        both_out[p, :rows] = (n_buf[p] * adapter_scale).T


def select(narrow, wide, index):
    experts = index.shape[0]
    _, projections, rank, rows = narrow.shape
    columns = wide.shape[3]
    deep = experts * rank
    return pl.pallas_call(
        select_kernel,
        out_shape=(
            jax.ShapeDtypeStruct((projections, rows + columns, deep), narrow.dtype),
            jax.ShapeDtypeStruct((projections, columns, deep), wide.dtype),
        ),
        in_specs=[in_hbm] * 3,
        out_specs=[in_vmem] * 2,
        scratch_shapes=[
            pltpu.SMEM((experts,), index.dtype),
            pltpu.VMEM((projections, deep, rows), narrow.dtype),
            pltpu.VMEM((projections, deep, columns), wide.dtype),
            pltpu.SemaphoreType.DMA,
            pltpu.SemaphoreType.DMA((experts, 2)),
        ],
        compiler_params=pltpu.CompilerParams(vmem_limit_bytes=vmem_limit),
        name="select",
    )(*[pltpu.with_memory_space_constraint(x, pltpu.HBM) for x in (index, narrow, wide)])


def load_kernel(blocks, base_ref, *refs):
    out_ref, sems = refs[-2:]
    s = lax.axis_index("shard")
    copies = []
    for n, (chunk, span, first, last) in enumerate(blocks):
        columns = pl.ds(pl.multiple_of(chunk(s) * span, span), span)
        rows = pl.ds(first, last - first)
        copies.append(
            pltpu.make_async_copy(base_ref.at[:, :, rows, columns], out_ref.at[:, :, rows, columns], sems.at[n])
        )
    for copy in copies:
        copy.start()
    for copy in copies:
        copy.wait()


def load(base, blocks, after, held=None):
    operands = [pltpu.with_memory_space_constraint(base, pltpu.HBM), after] + ([] if held is None else [held])
    return pl.pallas_call(
        functools.partial(load_kernel, blocks),
        out_shape=jax.ShapeDtypeStruct(base.shape, base.dtype),
        in_specs=[in_hbm, anywhere, in_vmem][: len(operands)],
        out_specs=in_vmem,
        scratch_shapes=[pltpu.SemaphoreType.DMA((len(blocks),))],
        input_output_aliases={} if held is None else {2: 0},
        compiler_params=pltpu.CompilerParams(vmem_limit_bytes=vmem_limit),
        cost_estimate=pl.CostEstimate(flops=0, bytes_accessed=2 * base.size, transcendentals=0),
        name="load",
    )(*operands)


def pack_kernel(count, *refs):
    out_ref = refs[-1]
    at = 0
    for ref in refs[:count]:
        rows = ref.shape[1]
        out_ref[:, at : at + rows] = ref[...]
        at += rows


def pack(blocks, after=()):
    projections, _, deep = blocks[0].shape
    rows = sum(x.shape[1] for x in blocks)
    return pl.pallas_call(
        functools.partial(pack_kernel, len(blocks)),
        out_shape=jax.ShapeDtypeStruct((projections, rows, deep), blocks[0].dtype),
        in_specs=[in_vmem] * len(blocks) + [anywhere] * len(after),
        out_specs=in_vmem,
        compiler_params=pltpu.CompilerParams(vmem_limit_bytes=vmem_limit),
        name="pack",
    )(*blocks, *after)


def merge_kernel(plan, held_ref, *refs):
    out_ref, token, n_all, w_all, out_buf, sems = refs[-6:]
    experts, projections, width, _ = held_ref.shape
    _, span, deep = w_all.shape
    m_step = tile_rows if width % tile_rows == 0 else width
    f_step = 256 if span % 256 == 0 else span
    steps = projections * experts
    s, g = lax.axis_index("shard"), lax.axis_index("group")
    lane_expert = lax.broadcasted_iota(jnp.int32, (m_step, deep), 1) // plan.rank

    def prepare(p):
        for i, first, rows, place in plan.n_pieces:
            at = pl.multiple_of(place(s, g) * rows, rows)
            n_all[p, pl.ds(at, rows), :] = refs[i][p, pl.ds(first, rows)]
        for i, first, rows, place in plan.w_pieces:
            at = pl.multiple_of(place(s, g) * rows, rows)
            w_all[p, pl.ds(at, rows), :] = refs[i][p, pl.ds(first, rows)]

    def merge_chunk(first_column):
        columns = pl.ds(first_column, span)

        def out_copies(step):
            p, e = step // experts, lax.rem(step, experts)
            slot = lax.rem(step, out_slots)
            return [
                pltpu.make_async_copy(
                    out_buf.at[slot, pl.ds(m, m_step)],
                    out_ref.at[e, p, pl.ds(m, m_step), columns],
                    sems.at[slot, m // m_step],
                )
                for m in range(0, width, m_step)
            ]

        def tile(step, _):
            p, e = step // experts, lax.rem(step, experts)
            slot = lax.rem(step, out_slots)
            pl.when(e == 0)(lambda: prepare(p))

            @pl.when(step >= out_slots)
            def _():
                for copy in out_copies(step - out_slots):
                    copy.wait()

            for copy, m in zip(out_copies(step), range(0, width, m_step)):
                n = n_all[p, m : m + m_step, :]
                n = jnp.where(lane_expert == e, n, jnp.zeros_like(n))
                for f in range(0, span, f_step):
                    delta = lax.dot_general(
                        n, w_all[p, f : f + f_step], (((1,), (1,)), ((), ())), preferred_element_type=jnp.float32
                    )
                    b = held_ref[e, p, m : m + m_step, first_column + f : first_column + f + f_step]
                    out_buf[slot, m : m + m_step, f : f + f_step] = (b.astype(jnp.float32) + delta).astype(out_buf.dtype)
                copy.start()
            return 0

        lax.fori_loop(0, steps, tile, 0)
        for step in range(max(0, steps - out_slots), steps):
            for copy in out_copies(jnp.int32(step)):
                copy.wait()

    for c in range(plan.chunks):
        pl.when(plan.chunk(s) == c)(functools.partial(merge_chunk, c * span))
    token[...] = jnp.zeros_like(token)


class Plan(typing.NamedTuple):
    rank: int
    span: int
    chunks: int
    chunk: typing.Callable
    n_pieces: list
    w_pieces: list


def merge(plan, held, parts, out=None, after=()):
    experts, projections, width, _ = held.shape
    deep = parts[0].shape[-1]
    m_step = tile_rows if width % tile_rows == 0 else width
    share = projections * plan.span * experts * width
    extra = [*after] + ([] if out is None else [out])
    operands = [held, *parts, *extra]
    return pl.pallas_call(
        functools.partial(merge_kernel, plan),
        out_shape=[jax.ShapeDtypeStruct(held.shape, held.dtype), jax.ShapeDtypeStruct((8, 128), jnp.float32)],
        in_specs=[in_vmem] * (1 + len(parts)) + [anywhere] * len(extra),
        out_specs=[in_hbm, in_vmem],
        scratch_shapes=[
            pltpu.VMEM((projections, width, deep), held.dtype),
            pltpu.VMEM((projections, plan.span, deep), held.dtype),
            pltpu.VMEM((out_slots, width, plan.span), held.dtype),
            pltpu.SemaphoreType.DMA((out_slots, width // m_step)),
        ],
        input_output_aliases={} if out is None else {len(operands) - 1: 0},
        compiler_params=pltpu.CompilerParams(vmem_limit_bytes=vmem_limit),
        cost_estimate=pl.CostEstimate(flops=2 * share * plan.rank, bytes_accessed=4 * share, transcendentals=0),
        name="merge",
    )(*operands)


def on_device(shards, groups, base, narrow, wide, adapted_expert_index):
    rank = narrow.shape[3]
    rows, columns = narrow.shape[2], wide.shape[3]
    axes = ("shard", "group")
    narrow = jnp.swapaxes(narrow, 2, 3)

    if shards != 4 or groups != 4:
        both, w = select(narrow, wide, adapted_expert_index)
        n = lax.all_gather(both[:, :rows], "group", axis=1, tiled=True)
        w = lax.all_gather(w, axes, axis=1, tiled=True)
        whole = lambda s, g: 0
        n_pieces = [(0, 0, rows * groups, whole)]
        w_pieces = [(1, 0, columns * shards * groups, whole)]
        plan = Plan(rank, columns * shards * groups, 1, lambda s: 0, n_pieces, w_pieces)
        return merge(plan, base, [n, w])[0]

    def swap(x, axis, bit):
        return lax.ppermute(x, axis, [(i, i ^ bit) for i in range(4)])

    both, w = select(narrow, wide, adapted_expert_index)
    w3, w2, w1 = [swap(w, "shard", k) for k in (3, 2, 1)]
    width = base.shape[2]
    split = width * 14 // 16
    span = 2 * columns * groups
    near_half, far_half = lambda s: s // 2, lambda s: 1 - s // 2
    held = load(base, [(near_half, span, 0, width), (far_half, span, 0, split)], w1)
    line = pack([w2, w3], (held,))
    own_a = pack([both, swap(both, "group", 2), w1, swap(w1, "group", 2)], (line,))
    other_a = swap(own_a, "group", 1)
    line_x = swap(line, "group", 2)
    half = rows + columns
    n_pieces = [
        (i, first, rows, lambda s, g, m=m: g ^ m)
        for i, first, m in ((0, 0, 0), (0, half, 2), (1, 0, 1), (1, half, 3))
    ]

    def w_piece(i, first, k, m):
        return (i, first, columns, lambda s, g: ((s ^ k) % 2) * groups + (g ^ m))

    near, far = [], []
    for i, m in ((0, 0), (1, 1)):
        near += [w_piece(i, rows, 0, m), w_piece(i, half + rows, 0, m ^ 2)]
        near += [w_piece(i, 2 * half, 1, m), w_piece(i, 2 * half + columns, 1, m ^ 2)]
        for at, k in ((0, 2), (1, 3)):
            far += [w_piece(i + 2, at * columns, k, m), w_piece(i + 2, (at + 2) * columns, k, m ^ 2)]
    near_plan = Plan(rank, span, 2, near_half, n_pieces, near)
    far_plan = Plan(rank, span, 2, far_half, n_pieces, far)
    parts = [own_a, other_a]
    out, token = merge(near_plan, held, parts, after=(line,))
    own_b = pack([line, line_x], (token,))
    held = load(base, [(far_half, span, split, width)], own_b, held)
    return merge(far_plan, held, parts + [own_b, swap(own_b, "group", 1)], out)[0]


def solution(mesh):
    return jax.shard_map(
        functools.partial(on_device, mesh.shape["shard"], mesh.shape["group"]),
        mesh=mesh,
        in_specs=(
            P("parts", None, "shard", None),
            P("parts", None, ("shard", "group"), None),
            P("parts", None, None, ("shard", "group")),
            P("parts"),
        ),
        out_specs=P("parts", None, "shard", None),
        check_vma=False,
    )
```
